32 devices in a mesh: dp: 16 (over z, y, core), layer: 2 (over x).
Axes of the slice: x: 2, y: 2, z: 4, core: 2. Of those that a mesh axis runs over, the one named last changes fastest.
Arguments:
- query_inputs: bfloat16 [2, 16, 128, 4096], P('layer', 'dp'), may hold values from -6 to 6
- query_cotangents: bfloat16 [2, 16, 128, 4096], P('layer', 'dp'), may hold values from -6 to 6
- query_lengths: int32 [16], P('dp'), may hold values from 64 to 128, as said below
- proj_in: bfloat16 [2, 64, 4096], P('layer'), may hold values from -0.09375 to 0.09375
- proj_out: bfloat16 [2, 64, 4096], P('layer'), may hold values from -0.09375 to 0.09375
- out_factor: float32 [2, 64, 64], P('layer'), may hold values from -1 to 5, as said below
- in_factor: float32 [2, 64, 64], P('layer'), may hold values from -1 to 5, as said below
- train_grads: bfloat16 [2, 2048, 4096], P('layer', 'dp'), may hold values from -0.0009765625 to 0.0009765625
Outputs:
- scores: float32 [16, 2048], P('layer', 'dp')
The draws below stay inside these ranges and needn't reach their ends.
Inputs may be any that keep to these rules, and one draw needn't show every extreme that they name: `query_lengths`: some query sequence has 128 valid tokens and some has 64. `out_factor`: each matrix is symmetric positive definite. `in_factor`: each matrix is symmetric positive definite.
All inputs are finite; a program needn't handle non-finite values.
Results may differ from the reference program's by a relative error of at most 0.0057.
Values may be sent and summed in bfloat16 or wider, within the bound.
A program may use at most 64 MiB of HBM per device.

```python
import math
import jax
import jax.numpy as jnp
from jax import lax

D = 4096
RANK = 64
LEN = 128
BLOCKS = 2
QUERIES = 16
TRAIN_SEQUENCES = 2048


def draw_query_lengths(key, part):
    key = jax.random.fold_in(key, 5)
    drawn = jax.random.randint(key, (QUERIES,), LEN // 2, LEN + 1, dtype=jnp.int32)
    slots = jnp.arange(QUERIES, dtype=jnp.int32)
    drawn = jnp.where(slots == 0, LEN, drawn)
    return jnp.where(slots == 1, LEN // 2, drawn)


def factor_matrix(key):
    first_key, second_key = jax.random.split(key)
    noise_draw = jax.random.normal(first_key, (BLOCKS, RANK, RANK), jnp.float32)
    symmetric = (noise_draw + jnp.swapaxes(noise_draw, 1, 2)) * (0.25 / math.sqrt(RANK))
    diagonal_entries = jnp.exp(jax.random.uniform(second_key, (BLOCKS, RANK), jnp.float32, 0.0, math.log(4.0)))
    return symmetric + jnp.eye(RANK, dtype=jnp.float32)[None, :, :] * diagonal_entries[:, None, :]


def draw_out_factor(key, part):
    key = jax.random.fold_in(key, 7)
    return factor_matrix(key)


def draw_in_factor(key, part):
    key = jax.random.fold_in(key, 11)
    return factor_matrix(key)


def block_levels(stream_key, shape, cuts, smallest, largest):
    def one(axis_at, parts):
        steps = jax.random.uniform(jax.random.fold_in(jax.random.fold_in(stream_key, 6), axis_at), (parts,), jnp.float32, smallest / len(cuts), largest / len(cuts))
        return jnp.repeat(jnp.exp(steps), shape[axis_at] // parts).reshape((-1,) + (1,) * (len(shape) - axis_at - 1))

    loudness = one(*cuts[0])
    for cut in cuts[1:]:
        loudness = loudness * one(*cut)
    return loudness


def bell_draw(own_key, extent, spread, most, pieces=(), held_as=jnp.bfloat16):
    values = spread * jax.random.normal(own_key, extent, jnp.float32)
    if pieces:
        values = values * block_levels(own_key, extent, pieces, -0.22, 0.18)
    return jnp.clip(values, -most, most).astype(held_as)


def setup_inputs(seed: int = 0) -> dict:
    key_of = jax.random.split(jax.random.key(seed), 9)
    return {
        "query_inputs": bell_draw(key_of[0], (BLOCKS, QUERIES, LEN, D), 1.0, 6.0, ((0, 2), (1, 16))),
        "query_cotangents": bell_draw(key_of[1], (BLOCKS, QUERIES, LEN, D), 1.0, 6.0, ((0, 2), (1, 16))),
        "query_lengths": draw_query_lengths(jax.random.fold_in(key_of[8], 71), 0),
        "proj_in": bell_draw(key_of[3], (BLOCKS, RANK, D), D ** -0.5, 0.09375, ((0, 2),)),
        "proj_out": bell_draw(key_of[4], (BLOCKS, RANK, D), D ** -0.5, 0.09375, ((0, 2),)),
        "out_factor": draw_out_factor(jax.random.fold_in(key_of[8], 71), 0),
        "in_factor": draw_in_factor(jax.random.fold_in(key_of[8], 71), 0),
        "train_grads": bell_draw(key_of[7], (BLOCKS, TRAIN_SEQUENCES, RANK * RANK), (RANK * RANK * LEN * 64) ** -0.5, 0.0009765625, ((0, 2), (1, 16))),
    }


def reference(query_inputs, query_cotangents, query_lengths, proj_in, proj_out, out_factor, in_factor, train_grads):
    slots = jnp.arange(LEN, dtype=jnp.int32)
    valid = slots[None, :] < query_lengths[:, None]

    def one_block(operands):
        inputs, output_cotangents, side_in, side_out, left_kronecker, right_factor, logged = operands
        out_side = jnp.einsum("qld,rd->qlr", output_cotangents.astype(jnp.float32), side_out.astype(jnp.float32))
        out_side = jnp.where(valid[:, :, None], out_side, 0.0).astype(jnp.bfloat16)
        in_side = jnp.einsum("qld,rd->qlr", inputs.astype(jnp.float32), side_in.astype(jnp.float32)).astype(jnp.bfloat16)
        query_gradient_rows = jnp.einsum("qlr,qls->qrs", out_side.astype(jnp.float32), in_side.astype(jnp.float32)).astype(jnp.bfloat16)
        left_projection = jnp.einsum("ye,dei->dyi", left_kronecker, query_gradient_rows.astype(jnp.float32), precision=lax.Precision.HIGHEST)
        both_sides = jnp.einsum("qrs,st->qrt", left_projection, right_factor, precision=lax.Precision.HIGHEST)
        conditioned = both_sides.astype(jnp.bfloat16).reshape(QUERIES, RANK * RANK)
        return jnp.dot(conditioned, logged.T, preferred_element_type=jnp.float32)

    partials = lax.map(one_block, (query_inputs, query_cotangents, proj_in, proj_out, out_factor, in_factor, train_grads))
    return jnp.sum(partials, axis=0)
```

```python
import functools

import jax
import jax.numpy as jnp
from jax import lax
from jax.experimental import pallas as pl
from jax.experimental.pallas import tpu as pltpu
from jax.sharding import PartitionSpec as P

MESH = pl.DeviceIdType.MESH
F32 = jnp.float32
BF16 = jnp.bfloat16
NT = (((1,), (1,)), ((), ()))
CHUNKS = 4


def split(x):
    high = x.astype(BF16).astype(F32)
    return high, x - high


def dot_nt(a, b):
    return lax.dot_general(a, b, NT, preferred_element_type=F32)


def kernel(
    n,
    m,
    inputs_hbm,
    cotangents_hbm,
    lengths_hbm,
    proj_in_hbm,
    proj_out_hbm,
    out_factor_hbm,
    in_factor_hbm,
    train_hbm,
    out_ref,
    inputs,
    cotangents,
    length,
    proj_in,
    proj_out,
    out_factor,
    in_factor,
    train,
    weights,
    own,
    gathered,
    wide,
    partial,
    arrived,
    load_sem,
    small_sem,
    send_sem,
    recv_sem,
    layer_send_sem,
    layer_recv_sem,
):
    me = lax.axis_index("dp")
    layer = lax.axis_index("layer")
    tokens, width = inputs.shape
    rank = proj_in.shape[0]
    step = width // CHUNKS

    def load(sem, src, dst):
        copy = pltpu.make_async_copy(src, dst, sem)
        copy.start()
        return copy

    def columns(c):
        return pl.ds(c * step, step)

    out_loads = []
    in_loads = []
    for c in range(CHUNKS):
        out_loads.append(
            (
                load(load_sem.at[0, c], proj_out_hbm.at[0, :, columns(c)], proj_out.at[:, columns(c)]),
                load(load_sem.at[1, c], cotangents_hbm.at[0, 0, :, columns(c)], cotangents.at[:, columns(c)]),
            )
        )
    out_factor_load = load(small_sem.at[0], out_factor_hbm.at[0], out_factor)
    in_factor_load = load(small_sem.at[1], in_factor_hbm.at[0], in_factor)
    length_load = load(small_sem.at[2], lengths_hbm, length)
    for c in range(CHUNKS):
        in_loads.append(
            (
                load(load_sem.at[2, c], proj_in_hbm.at[0, :, columns(c)], proj_in.at[:, columns(c)]),
                load(load_sem.at[3, c], inputs_hbm.at[0, 0, :, columns(c)], inputs.at[:, columns(c)]),
            )
        )
    train_load = load(small_sem.at[3], train_hbm.at[0], train)

    barrier = pltpu.get_barrier_semaphore()
    peers = [lax.rem(me + k, n) for k in range(1, n)]
    layers = [lax.rem(layer + k, m) for k in range(1, m)]
    for peer in peers:
        pl.semaphore_signal(barrier, inc=1, device_id=(peer, layer), device_id_type=MESH)
    for other in layers:
        pl.semaphore_signal(barrier, inc=1, device_id=(me, other), device_id_type=MESH)

    out_factor_load.wait()
    in_factor_load.wait()
    half = rank // 2
    pair = 2 * rank
    factor_rows = jnp.concatenate(
        [out_factor[pl.ds(0, half, stride=2), :], out_factor[pl.ds(1, half, stride=2), :]], axis=1
    )
    left = jnp.concatenate(split(factor_rows), axis=1).astype(BF16)
    in_high, in_low = split(in_factor[...])
    none = jnp.zeros((rank, rank), F32)
    top = jnp.concatenate([in_high, none, in_low, none], axis=1)
    bottom = jnp.concatenate([none, in_high, none, in_low], axis=1)
    weights[...] = jnp.concatenate([top, bottom, top, bottom], axis=0).astype(BF16)

    def project(loads, proj, values):
        total = None
        for c in range(CHUNKS):
            for copy in loads[c]:
                copy.wait()
            term = dot_nt(proj[:, columns(c)], values[:, columns(c)])
            total = term if total is None else total + term
        return total

    out_side = project(out_loads, proj_out, cotangents)
    length_load.wait()
    slots = lax.broadcasted_iota(jnp.int32, (rank, tokens), 1)
    out_side = jnp.where(slots < length[0], out_side, 0.0)
    in_side = project(in_loads, proj_in, inputs)
    out_twice = jnp.concatenate([out_side, out_side], axis=0).astype(BF16)
    in_twice = jnp.concatenate([in_side, in_side], axis=0).astype(BF16)
    grads = dot_nt(out_twice, in_twice)
    rows = lax.broadcasted_iota(jnp.int32, (pair, pair), 0) < rank
    cols = lax.broadcasted_iota(jnp.int32, (pair, pair), 1) < rank
    grads = jnp.where(rows == cols, grads, 0.0).astype(BF16)
    projected = jnp.dot(left, jnp.concatenate([grads, grads], axis=0), preferred_element_type=F32)
    projected = jnp.concatenate(split(projected), axis=1).astype(BF16)
    both = jnp.dot(projected, weights[...], preferred_element_type=F32)
    own[...] = (both[:, :pair] + both[:, pair:]).astype(BF16)

    pl.semaphore_wait(barrier, n - 1 + m - 1)
    sends = []
    for k in range(1, n):
        copy = pltpu.make_async_remote_copy(
            src_ref=own,
            dst_ref=gathered.at[me],
            send_sem=send_sem.at[k],
            recv_sem=recv_sem.at[me],
            device_id=(peers[k - 1], layer),
            device_id_type=MESH,
        )
        copy.start()
        sends.append(copy)
    gathered[me] = own[...]
    train_load.wait()
    for k in range(1, n):
        source = lax.rem(me + n - k, n)
        pltpu.make_async_remote_copy(
            src_ref=own,
            dst_ref=gathered.at[source],
            send_sem=send_sem.at[k],
            recv_sem=recv_sem.at[source],
            device_id=(peers[k - 1], layer),
            device_id_type=MESH,
        ).wait_recv()

    wide[...] = gathered[...].astype(F32).reshape(wide.shape)
    conditioned = jnp.concatenate(
        [wide[pl.ds(j, n, stride=half), :] for j in range(half)], axis=1
    ).astype(BF16)
    scores = dot_nt(conditioned, train[...])
    partial[...] = scores.reshape(partial.shape)
    layer_sends = []
    for k in range(1, m):
        copy = pltpu.make_async_remote_copy(
            src_ref=partial.at[layers[k - 1]],
            dst_ref=arrived.at[k],
            send_sem=layer_send_sem.at[k],
            recv_sem=layer_recv_sem.at[k],
            device_id=(me, layers[k - 1]),
            device_id_type=MESH,
        )
        copy.start()
        layer_sends.append(copy)
    total = partial[layer]
    for copy in sends:
        copy.wait_send()
    for k in range(1, m):
        layer_sends[k - 1].wait_recv()
        total = total + arrived[k]
    out_ref[...] = total
    for copy in layer_sends:
        copy.wait_send()


def body(n, m, *args):
    inputs, _, lengths, proj_in, _, _, _, train = args
    _, _, tokens, width = inputs.shape
    rank = proj_in.shape[1]
    count = train.shape[1]
    rows = n // m
    half, pair = rank // 2, 2 * rank
    hbm = pl.BlockSpec(memory_space=pl.ANY)
    return pl.pallas_call(
        functools.partial(kernel, n, m),
        out_shape=jax.ShapeDtypeStruct((rows, count), F32),
        in_specs=[hbm] * len(args),
        out_specs=pl.BlockSpec(memory_space=pltpu.VMEM),
        scratch_shapes=[
            pltpu.VMEM((tokens, width), BF16),
            pltpu.VMEM((tokens, width), BF16),
            pltpu.SMEM((1,), jnp.int32),
            pltpu.VMEM((rank, width), BF16),
            pltpu.VMEM((rank, width), BF16),
            pltpu.VMEM((rank, rank), F32),
            pltpu.VMEM((rank, rank), F32),
            pltpu.VMEM((count, rank * rank), BF16),
            pltpu.VMEM((2 * pair, 2 * pair), BF16),
            pltpu.VMEM((half, pair), BF16),
            pltpu.VMEM((n, half, pair), BF16),
            pltpu.VMEM((n * half, pair), F32),
            pltpu.VMEM((m, rows, count), F32),
            pltpu.VMEM((m, rows, count), F32),
            pltpu.SemaphoreType.DMA((4, CHUNKS)),
            pltpu.SemaphoreType.DMA((4,)),
            pltpu.SemaphoreType.DMA((n,)),
            pltpu.SemaphoreType.DMA((n,)),
            pltpu.SemaphoreType.DMA((m,)),
            pltpu.SemaphoreType.DMA((m,)),
        ],
        compiler_params=pltpu.CompilerParams(
            collective_id=0, has_side_effects=True, vmem_limit_bytes=48 * 1024 * 1024
        ),
    )(*args)


def solution(mesh):
    n, m = mesh.shape["dp"], mesh.shape["layer"]
    in_specs = (
        P("layer", "dp", None, None),
        P("layer", "dp", None, None),
        P("dp"),
        P("layer", None, None),
        P("layer", None, None),
        P("layer", None, None),
        P("layer", None, None),
        P("layer", "dp", None),
    )
    return jax.shard_map(
        functools.partial(body, n, m),
        mesh=mesh,
        in_specs=in_specs,
        out_specs=P("layer", "dp"),
        check_vma=False,
    )
```

```python
import functools

import jax
import jax.numpy as jnp
from jax import lax
from jax.experimental import pallas as pl
from jax.experimental.pallas import tpu as pltpu
from jax.sharding import PartitionSpec as P

MESH = pl.DeviceIdType.MESH
F32 = jnp.float32
BF16 = jnp.bfloat16
NT = (((1,), (1,)), ((), ()))
CHUNKS = 4


def split(x):
    high = x.astype(BF16).astype(F32)
    return high, x - high


def dot_nt(a, b):
    return lax.dot_general(a, b, NT, preferred_element_type=F32)


def kernel(
    n,
    m,
    inputs_hbm,
    cotangents_hbm,
    lengths_hbm,
    proj_in_hbm,
    proj_out_hbm,
    out_factor_hbm,
    in_factor_hbm,
    train_hbm,
    out_ref,
    inputs,
    cotangents,
    length,
    proj_in,
    proj_out,
    out_factor,
    in_factor,
    train,
    weights,
    own,
    gathered,
    wide,
    partial,
    arrived,
    load_sem,
    small_sem,
    send_sem,
    recv_sem,
    layer_send_sem,
    layer_recv_sem,
):
    me = lax.axis_index("dp")
    layer = lax.axis_index("layer")
    tokens, width = inputs.shape
    rank = proj_in.shape[0]
    step = width // CHUNKS

    def load(sem, src, dst):
        copy = pltpu.make_async_copy(src, dst, sem)
        copy.start()
        return copy

    def columns(c):
        return pl.ds(c * step, step)

    out_loads = []
    in_loads = []
    for c in range(CHUNKS):
        out_loads.append(
            (
                load(load_sem.at[0, c], proj_out_hbm.at[0, :, columns(c)], proj_out.at[:, columns(c)]),
                load(load_sem.at[1, c], cotangents_hbm.at[0, 0, :, columns(c)], cotangents.at[:, columns(c)]),
            )
        )
    out_factor_load = load(small_sem.at[0], out_factor_hbm.at[0], out_factor)
    in_factor_load = load(small_sem.at[1], in_factor_hbm.at[0], in_factor)
    length_load = load(small_sem.at[2], lengths_hbm, length)
    for c in range(CHUNKS):
        in_loads.append(
            (
                load(load_sem.at[2, c], proj_in_hbm.at[0, :, columns(c)], proj_in.at[:, columns(c)]),
                load(load_sem.at[3, c], inputs_hbm.at[0, 0, :, columns(c)], inputs.at[:, columns(c)]),
            )
        )
    train_load = load(small_sem.at[3], train_hbm.at[0], train)

    barrier = pltpu.get_barrier_semaphore()
    peers = [lax.rem(me + k, n) for k in range(1, n)]
    layers = [lax.rem(layer + k, m) for k in range(1, m)]
    for peer in peers:
        pl.semaphore_signal(barrier, inc=1, device_id=(peer, layer), device_id_type=MESH)
    for other in layers:
        pl.semaphore_signal(barrier, inc=1, device_id=(me, other), device_id_type=MESH)

    out_factor_load.wait()
    in_factor_load.wait()
    half = rank // 2
    pair = 2 * rank
    factor_rows = jnp.concatenate(
        [out_factor[pl.ds(0, half, stride=2), :], out_factor[pl.ds(1, half, stride=2), :]], axis=1
    )
    left = jnp.concatenate(split(factor_rows), axis=1).astype(BF16)
    in_high, in_low = split(in_factor[...])
    none = jnp.zeros((rank, rank), F32)
    top = jnp.concatenate([in_high, none, in_low, none], axis=1)
    bottom = jnp.concatenate([none, in_high, none, in_low], axis=1)
    weights[...] = jnp.concatenate([top, bottom, top, bottom], axis=0).astype(BF16)

    def project(loads, proj, values):
        total = None
        for c in range(CHUNKS):
            for copy in loads[c]:
                copy.wait()
            term = dot_nt(proj[:, columns(c)], values[:, columns(c)])
            total = term if total is None else total + term
        return total

    out_side = project(out_loads, proj_out, cotangents)
    length_load.wait()
    slots = lax.broadcasted_iota(jnp.int32, (rank, tokens), 1)
    out_side = jnp.where(slots < length[0], out_side, 0.0)
    in_side = project(in_loads, proj_in, inputs)
    out_twice = jnp.concatenate([out_side, out_side], axis=0).astype(BF16)
    in_twice = jnp.concatenate([in_side, in_side], axis=0).astype(BF16)
    grads = dot_nt(out_twice, in_twice)
    rows = lax.broadcasted_iota(jnp.int32, (pair, pair), 0) < rank
    cols = lax.broadcasted_iota(jnp.int32, (pair, pair), 1) < rank
    grads = jnp.where(rows == cols, grads, 0.0).astype(BF16)
    projected = jnp.dot(left, jnp.concatenate([grads, grads], axis=0), preferred_element_type=F32)
    projected = jnp.concatenate(split(projected), axis=1).astype(BF16)
    both = jnp.dot(projected, weights[...], preferred_element_type=F32)
    own[...] = (both[:, :pair] + both[:, pair:]).astype(BF16)

    pl.semaphore_wait(barrier, n - 1 + m - 1)
    sends = []
    for k in range(1, n):
        copy = pltpu.make_async_remote_copy(
            src_ref=own,
            dst_ref=gathered.at[me],
            send_sem=send_sem.at[k],
            recv_sem=recv_sem.at[me],
            device_id=(peers[k - 1], layer),
            device_id_type=MESH,
        )
        copy.start()
        sends.append(copy)
    gathered[me] = own[...]
    train_load.wait()
    for k in range(1, n):
        source = lax.rem(me + n - k, n)
        pltpu.make_async_remote_copy(
            src_ref=own,
            dst_ref=gathered.at[source],
            send_sem=send_sem.at[k],
            recv_sem=recv_sem.at[source],
            device_id=(peers[k - 1], layer),
            device_id_type=MESH,
        ).wait_recv()

    wide[...] = gathered[...].astype(F32).reshape(wide.shape)
    conditioned = jnp.concatenate(
        [wide[pl.ds(j, n, stride=half), :] for j in range(half)], axis=1
    ).astype(BF16)
    scores = dot_nt(conditioned, train[...])
    partial[...] = scores.reshape(partial.shape)
    layer_sends = []
    for k in range(1, m):
        copy = pltpu.make_async_remote_copy(
            src_ref=partial.at[layers[k - 1]],
            dst_ref=arrived.at[k],
            send_sem=layer_send_sem.at[k],
            recv_sem=layer_recv_sem.at[k],
            device_id=(me, layers[k - 1]),
            device_id_type=MESH,
        )
        copy.start()
        layer_sends.append(copy)
    total = partial[layer]
    for copy in sends:
        copy.wait_send()
    for k in range(1, m):
        layer_sends[k - 1].wait_recv()
        total = total + arrived[k]
    out_ref[...] = total
    for copy in layer_sends:
        copy.wait_send()


def body(n, m, *args):
    inputs, _, lengths, proj_in, _, _, _, train = args
    _, _, tokens, width = inputs.shape
    rank = proj_in.shape[1]
    count = train.shape[1]
    rows = n // m
    half, pair = rank // 2, 2 * rank
    hbm = pl.BlockSpec(memory_space=pltpu.HBM)
    return pl.pallas_call(
        functools.partial(kernel, n, m),
        out_shape=jax.ShapeDtypeStruct((rows, count), F32),
        in_specs=[hbm] * len(args),
        out_specs=pl.BlockSpec(memory_space=pltpu.VMEM),
        scratch_shapes=[
            pltpu.VMEM((tokens, width), BF16),
            pltpu.VMEM((tokens, width), BF16),
            pltpu.SMEM((1,), jnp.int32),
            pltpu.VMEM((rank, width), BF16),
            pltpu.VMEM((rank, width), BF16),
            pltpu.VMEM((rank, rank), F32),
            pltpu.VMEM((rank, rank), F32),
            pltpu.VMEM((count, rank * rank), BF16),
            pltpu.VMEM((2 * pair, 2 * pair), BF16),
            pltpu.VMEM((half, pair), BF16),
            pltpu.VMEM((n, half, pair), BF16),
            pltpu.VMEM((n * half, pair), F32),
            pltpu.VMEM((m, rows, count), F32),
            pltpu.VMEM((m, rows, count), F32),
            pltpu.SemaphoreType.DMA((4, CHUNKS)),
            pltpu.SemaphoreType.DMA((4,)),
            pltpu.SemaphoreType.DMA((n,)),
            pltpu.SemaphoreType.DMA((n,)),
            pltpu.SemaphoreType.DMA((m,)),
            pltpu.SemaphoreType.DMA((m,)),
        ],
        compiler_params=pltpu.CompilerParams(
            collective_id=0, has_side_effects=True, vmem_limit_bytes=63 * 1024 * 1024
        ),
    )(*args)


def solution(mesh):
    n, m = mesh.shape["dp"], mesh.shape["layer"]
    in_specs = (
        P("layer", "dp", None, None),
        P("layer", "dp", None, None),
        P("dp"),
        P("layer", None, None),
        P("layer", None, None),
        P("layer", None, None),
        P("layer", None, None),
        P("layer", "dp", None),
    )
    return jax.shard_map(
        functools.partial(body, n, m),
        mesh=mesh,
        in_specs=in_specs,
        out_specs=P("layer", "dp"),
        check_vma=False,
    )
```

```python
import functools

import jax
import jax.numpy as jnp
from jax import lax
from jax.experimental import pallas as pl
from jax.experimental.pallas import tpu as pltpu
from jax.sharding import PartitionSpec as P

MESH = pl.DeviceIdType.MESH
F32 = jnp.float32
BF16 = jnp.bfloat16
NT = (((1,), (1,)), ((), ()))
CHUNKS = 4


def split(x):
    high = x.astype(BF16).astype(F32)
    return high, x - high


def dot_nt(a, b):
    return lax.dot_general(a, b, NT, preferred_element_type=F32)


def kernel(
    n,
    m,
    inputs_hbm,
    cotangents_hbm,
    length,
    proj_in_hbm,
    proj_out_hbm,
    out_factor_hbm,
    in_factor_hbm,
    train_hbm,
    out_ref,
    inputs,
    cotangents,
    proj_in,
    proj_out,
    out_factor,
    in_factor,
    train,
    weights,
    own,
    gathered,
    wide,
    partial,
    arrived,
    load_sem,
    small_sem,
    train_sem,
    send_sem,
    recv_sem,
    layer_send_sem,
    layer_recv_sem,
):
    me = lax.axis_index("dp")
    layer = lax.axis_index("layer")
    tokens, width = inputs.shape
    rank = proj_in.shape[0]
    step = width // CHUNKS

    def load(sem, src, dst):
        copy = pltpu.make_async_copy(src, dst, sem)
        copy.start()
        return copy

    def columns(c):
        return pl.ds(c * step, step)

    out_loads = []
    in_loads = []
    for c in range(CHUNKS):
        out_loads.append(
            (
                load(load_sem.at[0, c], proj_out_hbm.at[0, :, columns(c)], proj_out.at[:, columns(c)]),
                load(load_sem.at[1, c], cotangents_hbm.at[0, 0, :, columns(c)], cotangents.at[:, columns(c)]),
            )
        )
    out_factor_load = load(small_sem.at[0], out_factor_hbm.at[0], out_factor)
    in_factor_load = load(small_sem.at[1], in_factor_hbm.at[0], in_factor)
    for c in range(CHUNKS):
        in_loads.append(
            (
                load(load_sem.at[2, c], proj_in_hbm.at[0, :, columns(c)], proj_in.at[:, columns(c)]),
                load(load_sem.at[3, c], inputs_hbm.at[0, 0, :, columns(c)], inputs.at[:, columns(c)]),
            )
        )
    core = lax.rem(me, 2)
    sibling = me + 1 - 2 * core
    train_load = load(small_sem.at[2], train_hbm.at[0], train.at[core])

    barrier = pltpu.get_barrier_semaphore()
    peers = [lax.rem(me + 2 * k, n) for k in range(1, n // 2)]
    layers = [lax.rem(layer + k, m) for k in range(1, m)]
    partners = [(sibling, layer)] + [(dp, other) for other in layers for dp in (me, sibling)]
    greeted = [(peer, layer) for peer in peers] + partners
    for device in greeted:
        pl.semaphore_signal(barrier, inc=1, device_id=device, device_id_type=MESH)

    out_factor_load.wait()
    in_factor_load.wait()
    half = rank // 2
    pair = 2 * rank
    factor_rows = jnp.concatenate(
        [out_factor[pl.ds(0, half, stride=2), :], out_factor[pl.ds(1, half, stride=2), :]], axis=1
    )
    left = jnp.concatenate(split(factor_rows), axis=1).astype(BF16)
    in_high, in_low = split(in_factor[...])
    none = jnp.zeros((rank, rank), F32)
    top = jnp.concatenate([in_high, none, in_low, none], axis=1)
    bottom = jnp.concatenate([none, in_high, none, in_low], axis=1)
    weights[...] = jnp.concatenate([top, bottom, top, bottom], axis=0).astype(BF16)

    def project(loads, proj, values):
        total = None
        for c in range(CHUNKS):
            for copy in loads[c]:
                copy.wait()
            term = dot_nt(proj[:, columns(c)], values[:, columns(c)])
            total = term if total is None else total + term
        return total

    out_side = project(out_loads, proj_out, cotangents)
    slots = lax.broadcasted_iota(jnp.int32, (rank, tokens), 1)
    out_side = jnp.where(slots < length[0], out_side, 0.0)
    pl.semaphore_wait(barrier, len(greeted))
    train_share = pltpu.make_async_remote_copy(
        src_ref=train_hbm.at[0],
        dst_ref=train.at[core],
        send_sem=train_sem.at[0],
        recv_sem=train_sem.at[1],
        device_id=(sibling, layer),
        device_id_type=MESH,
    )
    train_share.start()
    in_side = project(in_loads, proj_in, inputs)
    out_twice = jnp.concatenate([out_side, out_side], axis=0).astype(BF16)
    in_twice = jnp.concatenate([in_side, in_side], axis=0).astype(BF16)
    grads = dot_nt(out_twice, in_twice)
    rows = lax.broadcasted_iota(jnp.int32, (pair, pair), 0) < rank
    cols = lax.broadcasted_iota(jnp.int32, (pair, pair), 1) < rank
    grads = jnp.where(rows == cols, grads, 0.0).astype(BF16)
    projected = jnp.dot(left, jnp.concatenate([grads, grads], axis=0), preferred_element_type=F32)
    projected = jnp.concatenate(split(projected), axis=1).astype(BF16)
    both = jnp.dot(projected, weights[...], preferred_element_type=F32)
    own[...] = (both[:, :pair] + both[:, pair:]).astype(BF16)

    place = me // 2
    sends = []
    for k, peer in enumerate(peers):
        copy = pltpu.make_async_remote_copy(
            src_ref=own,
            dst_ref=gathered.at[place],
            send_sem=send_sem.at[k],
            recv_sem=recv_sem.at[place],
            device_id=(peer, layer),
            device_id_type=MESH,
        )
        copy.start()
        sends.append(copy)
    gathered[place] = own[...]
    train_load.wait()
    pltpu.make_async_remote_copy(
        src_ref=train_hbm.at[0],
        dst_ref=train.at[1 - core],
        send_sem=train_sem.at[0],
        recv_sem=train_sem.at[1],
        device_id=(sibling, layer),
        device_id_type=MESH,
    ).wait_recv()
    for k, peer in enumerate(peers):
        source = peer // 2
        pltpu.make_async_remote_copy(
            src_ref=own,
            dst_ref=gathered.at[source],
            send_sem=send_sem.at[k],
            recv_sem=recv_sem.at[source],
            device_id=(peer, layer),
            device_id_type=MESH,
        ).wait_recv()

    wide[...] = gathered[...].astype(F32).reshape(wide.shape)
    conditioned = jnp.concatenate(
        [wide[pl.ds(j, n // 2, stride=half), :] for j in range(half)], axis=1
    ).astype(BF16)
    scores = dot_nt(conditioned, train[...].reshape(2 * train.shape[1], train.shape[2]))
    _, _, rows, count = partial.shape
    for other in range(m):
        for c in range(2):
            partial[other, c] = scores[other * rows : (other + 1) * rows, c * count : (c + 1) * count]
    results = []
    for k, (dp, other) in enumerate(partners):
        copy = pltpu.make_async_remote_copy(
            src_ref=partial.at[other, lax.rem(dp, 2)],
            dst_ref=arrived.at[layer, core],
            send_sem=layer_send_sem.at[k],
            recv_sem=layer_recv_sem.at[layer, core],
            device_id=(dp, other),
            device_id_type=MESH,
        )
        copy.start()
        results.append(copy)
    arrived[layer, core] = partial[layer, core]
    train_share.wait_send()
    for copy in sends:
        copy.wait_send()
    for k, (dp, other) in enumerate(partners):
        pltpu.make_async_remote_copy(
            src_ref=partial.at[other, lax.rem(dp, 2)],
            dst_ref=arrived.at[other, lax.rem(dp, 2)],
            send_sem=layer_send_sem.at[k],
            recv_sem=layer_recv_sem.at[other, lax.rem(dp, 2)],
            device_id=(dp, other),
            device_id_type=MESH,
        ).wait_recv()
    for c in range(2):
        total = arrived[0, c]
        for other in range(1, m):
            total = total + arrived[other, c]
        out_ref[pl.ds(c, rows, stride=2), :] = total
    for copy in results:
        copy.wait_send()


def body(n, m, *args):
    inputs, _, _, proj_in, _, _, _, train = args
    _, _, tokens, width = inputs.shape
    rank = proj_in.shape[1]
    count = train.shape[1]
    rows = n // m
    half, pair = rank // 2, 2 * rank
    hbm = pl.BlockSpec(memory_space=pltpu.HBM)
    return pl.pallas_call(
        functools.partial(kernel, n, m),
        out_shape=jax.ShapeDtypeStruct((rows, count), F32),
        in_specs=[hbm, hbm, pl.BlockSpec(memory_space=pltpu.SMEM)] + [hbm] * 5,
        out_specs=pl.BlockSpec(memory_space=pltpu.VMEM),
        scratch_shapes=[
            pltpu.VMEM((tokens, width), BF16),
            pltpu.VMEM((tokens, width), BF16),
            pltpu.VMEM((rank, width), BF16),
            pltpu.VMEM((rank, width), BF16),
            pltpu.VMEM((rank, rank), F32),
            pltpu.VMEM((rank, rank), F32),
            pltpu.VMEM((2, count, rank * rank), BF16),
            pltpu.VMEM((2 * pair, 2 * pair), BF16),
            pltpu.VMEM((half, pair), BF16),
            pltpu.VMEM((n // 2, half, pair), BF16),
            pltpu.VMEM((n // 2 * half, pair), F32),
            pltpu.VMEM((m, 2, rows // 2, count), F32),
            pltpu.VMEM((m, 2, rows // 2, count), F32),
            pltpu.SemaphoreType.DMA((4, CHUNKS)),
            pltpu.SemaphoreType.DMA((3,)),
            pltpu.SemaphoreType.DMA((2,)),
            pltpu.SemaphoreType.DMA((n // 2,)),
            pltpu.SemaphoreType.DMA((n // 2,)),
            pltpu.SemaphoreType.DMA((2 * m,)),
            pltpu.SemaphoreType.DMA((m, 2)),
        ],
        compiler_params=pltpu.CompilerParams(
            collective_id=0, has_side_effects=True, vmem_limit_bytes=55212 * 1024
        ),
    )(*args)


def solution(mesh):
    n, m = mesh.shape["dp"], mesh.shape["layer"]
    in_specs = (
        P("layer", "dp", None, None),
        P("layer", "dp", None, None),
        P("dp"),
        P("layer", None, None),
        P("layer", None, None),
        P("layer", None, None),
        P("layer", None, None),
        P("layer", "dp", None),
    )
    return jax.shard_map(
        functools.partial(body, n, m),
        mesh=mesh,
        in_specs=in_specs,
        out_specs=P("layer", "dp"),
        check_vma=False,
    )
```

```python
import functools

import jax
import jax.numpy as jnp
from jax import lax
from jax.experimental import pallas as pl
from jax.experimental.pallas import tpu as pltpu
from jax.sharding import PartitionSpec as P

MESH = pl.DeviceIdType.MESH
F32 = jnp.float32
BF16 = jnp.bfloat16
NT = (((1,), (1,)), ((), ()))
CHUNKS = 1


def split(x):
    high = x.astype(BF16).astype(F32)
    return high, x - high


def dot_nt(a, b):
    return lax.dot_general(a, b, NT, preferred_element_type=F32)


def kernel(
    n,
    m,
    inputs_hbm,
    cotangents_hbm,
    length,
    proj_in_hbm,
    proj_out_hbm,
    out_factor_hbm,
    in_factor_hbm,
    train_hbm,
    out_ref,
    inputs,
    cotangents,
    proj_in,
    proj_out,
    out_factor,
    in_factor,
    train,
    weights,
    own,
    gathered,
    wide,
    partial,
    arrived,
    load_sem,
    small_sem,
    train_sem,
    send_sem,
    recv_sem,
    layer_send_sem,
    layer_recv_sem,
):
    me = lax.axis_index("dp")
    layer = lax.axis_index("layer")
    tokens, width = inputs.shape
    rank = proj_in.shape[0]
    step = width // CHUNKS

    def load(sem, src, dst):
        copy = pltpu.make_async_copy(src, dst, sem)
        copy.start()
        return copy

    def columns(c):
        return pl.ds(c * step, step)

    out_loads = []
    in_loads = []
    for c in range(CHUNKS):
        out_loads.append(
            (
                load(load_sem.at[0, c], proj_out_hbm.at[0, :, columns(c)], proj_out.at[:, columns(c)]),
                load(load_sem.at[1, c], cotangents_hbm.at[0, 0, :, columns(c)], cotangents.at[:, columns(c)]),
            )
        )
    out_factor_load = load(small_sem.at[0], out_factor_hbm.at[0], out_factor)
    in_factor_load = load(small_sem.at[1], in_factor_hbm.at[0], in_factor)
    for c in range(CHUNKS):
        in_loads.append(
            (
                load(load_sem.at[2, c], proj_in_hbm.at[0, :, columns(c)], proj_in.at[:, columns(c)]),
                load(load_sem.at[3, c], inputs_hbm.at[0, 0, :, columns(c)], inputs.at[:, columns(c)]),
            )
        )
    core = lax.rem(me, 2)
    sibling = me + 1 - 2 * core
    train_load = load(small_sem.at[2], train_hbm.at[0], train.at[core])

    barrier = pltpu.get_barrier_semaphore()
    peers = [lax.rem(me + 2 * k, n) for k in range(1, n // 2)]
    layers = [lax.rem(layer + k, m) for k in range(1, m)]
    partners = [(sibling, layer)] + [(dp, other) for other in layers for dp in (me, sibling)]
    greeted = [(peer, layer) for peer in peers] + partners
    for device in greeted:
        pl.semaphore_signal(barrier, inc=1, device_id=device, device_id_type=MESH)

    pl.semaphore_wait(barrier, len(greeted))
    train_share = pltpu.make_async_remote_copy(
        src_ref=train_hbm.at[0],
        dst_ref=train.at[core],
        send_sem=train_sem.at[0],
        recv_sem=train_sem.at[1],
        device_id=(sibling, layer),
        device_id_type=MESH,
    )
    train_share.start()
    out_factor_load.wait()
    in_factor_load.wait()
    half = rank // 2
    pair = 2 * rank
    factor_rows = jnp.concatenate(
        [out_factor[pl.ds(0, half, stride=2), :], out_factor[pl.ds(1, half, stride=2), :]], axis=1
    )
    left = jnp.concatenate(split(factor_rows), axis=1).astype(BF16)
    in_high, in_low = split(in_factor[...])
    none = jnp.zeros((rank, rank), F32)
    top = jnp.concatenate([in_high, none, in_low, none], axis=1)
    bottom = jnp.concatenate([none, in_high, none, in_low], axis=1)
    weights[...] = jnp.concatenate([top, bottom, top, bottom], axis=0).astype(BF16)

    def project(loads, proj, values):
        total = None
        for c in range(CHUNKS):
            for copy in loads[c]:
                copy.wait()
            term = dot_nt(proj[:, columns(c)], values[:, columns(c)])
            total = term if total is None else total + term
        return total

    out_side = project(out_loads, proj_out, cotangents)
    slots = lax.broadcasted_iota(jnp.int32, (rank, tokens), 1)
    out_side = jnp.where(slots < length[0], out_side, 0.0)
    in_side = project(in_loads, proj_in, inputs)
    out_twice = jnp.concatenate([out_side, out_side], axis=0).astype(BF16)
    in_twice = jnp.concatenate([in_side, in_side], axis=0).astype(BF16)
    grads = dot_nt(out_twice, in_twice)
    rows = lax.broadcasted_iota(jnp.int32, (pair, pair), 0) < rank
    cols = lax.broadcasted_iota(jnp.int32, (pair, pair), 1) < rank
    grads = jnp.where(rows == cols, grads, 0.0).astype(BF16)
    projected = jnp.dot(left, jnp.concatenate([grads, grads], axis=0), preferred_element_type=F32)
    projected = jnp.concatenate(split(projected), axis=1).astype(BF16)
    both = jnp.dot(projected, weights[...], preferred_element_type=F32)
    own[...] = (both[:, :pair] + both[:, pair:]).astype(BF16)

    place = me // 2
    sends = []
    for k, peer in enumerate(peers):
        copy = pltpu.make_async_remote_copy(
            src_ref=own,
            dst_ref=gathered.at[place],
            send_sem=send_sem.at[k],
            recv_sem=recv_sem.at[place],
            device_id=(peer, layer),
            device_id_type=MESH,
        )
        copy.start()
        sends.append(copy)
    gathered[place] = own[...]
    train_load.wait()
    pltpu.make_async_remote_copy(
        src_ref=train_hbm.at[0],
        dst_ref=train.at[1 - core],
        send_sem=train_sem.at[0],
        recv_sem=train_sem.at[1],
        device_id=(sibling, layer),
        device_id_type=MESH,
    ).wait_recv()
    for k, peer in enumerate(peers):
        source = peer // 2
        pltpu.make_async_remote_copy(
            src_ref=own,
            dst_ref=gathered.at[source],
            send_sem=send_sem.at[k],
            recv_sem=recv_sem.at[source],
            device_id=(peer, layer),
            device_id_type=MESH,
        ).wait_recv()

    wide[...] = gathered[...].astype(F32).reshape(wide.shape)
    conditioned = jnp.concatenate(
        [wide[pl.ds(j, n // 2, stride=half), :] for j in range(half)], axis=1
    ).astype(BF16)
    scores = dot_nt(conditioned, train[...].reshape(2 * train.shape[1], train.shape[2]))
    _, _, rows, count = partial.shape
    for other in range(m):
        for c in range(2):
            partial[other, c] = scores[other * rows : (other + 1) * rows, c * count : (c + 1) * count]
    results = []
    for k, (dp, other) in enumerate(partners):
        copy = pltpu.make_async_remote_copy(
            src_ref=partial.at[other, lax.rem(dp, 2)],
            dst_ref=arrived.at[layer, core],
            send_sem=layer_send_sem.at[k],
            recv_sem=layer_recv_sem.at[layer, core],
            device_id=(dp, other),
            device_id_type=MESH,
        )
        copy.start()
        results.append(copy)
    arrived[layer, core] = partial[layer, core]
    train_share.wait_send()
    for copy in sends:
        copy.wait_send()
    for k, (dp, other) in enumerate(partners):
        pltpu.make_async_remote_copy(
            src_ref=partial.at[other, lax.rem(dp, 2)],
            dst_ref=arrived.at[other, lax.rem(dp, 2)],
            send_sem=layer_send_sem.at[k],
            recv_sem=layer_recv_sem.at[other, lax.rem(dp, 2)],
            device_id=(dp, other),
            device_id_type=MESH,
        ).wait_recv()
    for c in range(2):
        total = arrived[0, c]
        for other in range(1, m):
            total = total + arrived[other, c]
        out_ref[pl.ds(c, rows, stride=2), :] = total
    for copy in results:
        copy.wait_send()


def body(n, m, *args):
    inputs, _, _, proj_in, _, _, _, train = args
    _, _, tokens, width = inputs.shape
    rank = proj_in.shape[1]
    count = train.shape[1]
    rows = n // m
    half, pair = rank // 2, 2 * rank
    hbm = pl.BlockSpec(memory_space=pltpu.HBM)
    return pl.pallas_call(
        functools.partial(kernel, n, m),
        out_shape=jax.ShapeDtypeStruct((rows, count), F32),
        in_specs=[hbm, hbm, pl.BlockSpec(memory_space=pltpu.SMEM)] + [hbm] * 5,
        out_specs=pl.BlockSpec(memory_space=pltpu.VMEM),
        scratch_shapes=[
            pltpu.VMEM((tokens, width), BF16),
            pltpu.VMEM((tokens, width), BF16),
            pltpu.VMEM((rank, width), BF16),
            pltpu.VMEM((rank, width), BF16),
            pltpu.VMEM((rank, rank), F32),
            pltpu.VMEM((rank, rank), F32),
            pltpu.VMEM((2, count, rank * rank), BF16),
            pltpu.VMEM((2 * pair, 2 * pair), BF16),
            pltpu.VMEM((half, pair), BF16),
            pltpu.VMEM((n // 2, half, pair), BF16),
            pltpu.VMEM((n // 2 * half, pair), F32),
            pltpu.VMEM((m, 2, rows // 2, count), F32),
            pltpu.VMEM((m, 2, rows // 2, count), F32),
            pltpu.SemaphoreType.DMA((4, CHUNKS)),
            pltpu.SemaphoreType.DMA((3,)),
            pltpu.SemaphoreType.DMA((2,)),
            pltpu.SemaphoreType.DMA((n // 2,)),
            pltpu.SemaphoreType.DMA((n // 2,)),
            pltpu.SemaphoreType.DMA((2 * m,)),
            pltpu.SemaphoreType.DMA((m, 2)),
        ],
        compiler_params=pltpu.CompilerParams(
            collective_id=0, has_side_effects=True, vmem_limit_bytes=55212 * 1024
        ),
    )(*args)


def solution(mesh):
    n, m = mesh.shape["dp"], mesh.shape["layer"]
    in_specs = (
        P("layer", "dp", None, None),
        P("layer", "dp", None, None),
        P("dp"),
        P("layer", None, None),
        P("layer", None, None),
        P("layer", None, None),
        P("layer", None, None),
        P("layer", "dp", None),
    )
    return jax.shard_map(
        functools.partial(body, n, m),
        mesh=mesh,
        in_specs=in_specs,
        out_specs=P("layer", "dp"),
        check_vma=False,
    )
```

```python
import functools

import jax
import jax.numpy as jnp
from jax import lax
from jax.experimental import pallas as pl
from jax.experimental.pallas import tpu as pltpu
from jax.sharding import PartitionSpec as P

MESH = pl.DeviceIdType.MESH
F32 = jnp.float32
BF16 = jnp.bfloat16
NT = (((1,), (1,)), ((), ()))
CHUNKS = 1


def split(x):
    high = x.astype(BF16).astype(F32)
    return high, x - high


def dot_nt(a, b):
    return lax.dot_general(a, b, NT, preferred_element_type=F32)


def kernel(
    n,
    m,
    inputs_hbm,
    cotangents_hbm,
    length,
    proj_in_hbm,
    proj_out_hbm,
    out_factor_hbm,
    in_factor_hbm,
    train_hbm,
    out_ref,
    inputs,
    cotangents,
    proj_in,
    proj_out,
    out_factor,
    in_factor,
    train,
    weights,
    own,
    gathered,
    wide,
    partial,
    arrived,
    load_sem,
    small_sem,
    send_sem,
    recv_sem,
    layer_send_sem,
    layer_recv_sem,
):
    me = lax.axis_index("dp")
    layer = lax.axis_index("layer")
    tokens, width = inputs.shape
    rank = proj_in.shape[0]
    step = width // CHUNKS

    def load(sem, src, dst):
        copy = pltpu.make_async_copy(src, dst, sem)
        copy.start()
        return copy

    def columns(c):
        return pl.ds(c * step, step)

    out_loads = []
    in_loads = []
    for c in range(CHUNKS):
        out_loads.append(
            (
                load(load_sem.at[0, c], proj_out_hbm.at[0, :, columns(c)], proj_out.at[:, columns(c)]),
                load(load_sem.at[1, c], cotangents_hbm.at[0, 0, :, columns(c)], cotangents.at[:, columns(c)]),
            )
        )
    out_factor_load = load(small_sem.at[0], out_factor_hbm.at[0], out_factor)
    in_factor_load = load(small_sem.at[1], in_factor_hbm.at[0], in_factor)
    for c in range(CHUNKS):
        in_loads.append(
            (
                load(load_sem.at[2, c], proj_in_hbm.at[0, :, columns(c)], proj_in.at[:, columns(c)]),
                load(load_sem.at[3, c], inputs_hbm.at[0, 0, :, columns(c)], inputs.at[:, columns(c)]),
            )
        )
    train_load = load(small_sem.at[3], train_hbm.at[0], train)

    barrier = pltpu.get_barrier_semaphore()
    peers = [lax.rem(me + k, n) for k in range(1, n)]
    layers = [lax.rem(layer + k, m) for k in range(1, m)]
    for peer in peers:
        pl.semaphore_signal(barrier, inc=1, device_id=(peer, layer), device_id_type=MESH)
    for other in layers:
        pl.semaphore_signal(barrier, inc=1, device_id=(me, other), device_id_type=MESH)

    out_factor_load.wait()
    in_factor_load.wait()
    half = rank // 2
    pair = 2 * rank
    factor_rows = jnp.concatenate(
        [out_factor[pl.ds(0, half, stride=2), :], out_factor[pl.ds(1, half, stride=2), :]], axis=1
    )
    left = jnp.concatenate(split(factor_rows), axis=1).astype(BF16)
    in_high, in_low = split(in_factor[...])
    none = jnp.zeros((rank, rank), F32)
    top = jnp.concatenate([in_high, none, in_low, none], axis=1)
    bottom = jnp.concatenate([none, in_high, none, in_low], axis=1)
    weights[...] = jnp.concatenate([top, bottom, top, bottom], axis=0).astype(BF16)

    def project(loads, proj, values):
        total = None
        for c in range(CHUNKS):
            for copy in loads[c]:
                copy.wait()
            term = dot_nt(proj[:, columns(c)], values[:, columns(c)])
            total = term if total is None else total + term
        return total

    out_side = project(out_loads, proj_out, cotangents)
    slots = lax.broadcasted_iota(jnp.int32, (rank, tokens), 1)
    out_side = jnp.where(slots < length[0], out_side, 0.0)
    pl.semaphore_wait(barrier, n - 1 + m - 1)
    in_side = project(in_loads, proj_in, inputs)
    out_twice = jnp.concatenate([out_side, out_side], axis=0).astype(BF16)
    in_twice = jnp.concatenate([in_side, in_side], axis=0).astype(BF16)
    grads = dot_nt(out_twice, in_twice)
    rows = lax.broadcasted_iota(jnp.int32, (pair, pair), 0) < rank
    cols = lax.broadcasted_iota(jnp.int32, (pair, pair), 1) < rank
    grads = jnp.where(rows == cols, grads, 0.0).astype(BF16)
    projected = jnp.dot(left, jnp.concatenate([grads, grads], axis=0), preferred_element_type=F32)
    projected = jnp.concatenate(split(projected), axis=1).astype(BF16)
    both = jnp.dot(projected, weights[...], preferred_element_type=F32)
    own[...] = (both[:, :pair] + both[:, pair:]).astype(BF16)

    sends = []
    for k in range(1, n):
        copy = pltpu.make_async_remote_copy(
            src_ref=own,
            dst_ref=gathered.at[me],
            send_sem=send_sem.at[k],
            recv_sem=recv_sem.at[me],
            device_id=(peers[k - 1], layer),
            device_id_type=MESH,
        )
        copy.start()
        sends.append(copy)
    gathered[me] = own[...]
    train_load.wait()
    for k in range(1, n):
        source = lax.rem(me + n - k, n)
        pltpu.make_async_remote_copy(
            src_ref=own,
            dst_ref=gathered.at[source],
            send_sem=send_sem.at[k],
            recv_sem=recv_sem.at[source],
            device_id=(peers[k - 1], layer),
            device_id_type=MESH,
        ).wait_recv()

    wide[...] = gathered[...].astype(F32).reshape(wide.shape)
    conditioned = jnp.concatenate(
        [wide[pl.ds(j, n, stride=half), :] for j in range(half)], axis=1
    ).astype(BF16)
    scores = dot_nt(conditioned, train[...])
    partial[...] = scores.reshape(partial.shape)
    layer_sends = []
    for k in range(1, m):
        copy = pltpu.make_async_remote_copy(
            src_ref=partial.at[layers[k - 1]],
            dst_ref=arrived.at[k],
            send_sem=layer_send_sem.at[k],
            recv_sem=layer_recv_sem.at[k],
            device_id=(me, layers[k - 1]),
            device_id_type=MESH,
        )
        copy.start()
        layer_sends.append(copy)
    total = partial[layer]
    for copy in sends:
        copy.wait_send()
    for k in range(1, m):
        layer_sends[k - 1].wait_recv()
        total = total + arrived[k]
    out_ref[...] = total
    for copy in layer_sends:
        copy.wait_send()


def body(n, m, *args):
    inputs, _, _, proj_in, _, _, _, train = args
    _, _, tokens, width = inputs.shape
    rank = proj_in.shape[1]
    count = train.shape[1]
    rows = n // m
    half, pair = rank // 2, 2 * rank
    hbm = pl.BlockSpec(memory_space=pltpu.HBM)
    return pl.pallas_call(
        functools.partial(kernel, n, m),
        out_shape=jax.ShapeDtypeStruct((rows, count), F32),
        in_specs=[hbm, hbm, pl.BlockSpec(memory_space=pltpu.SMEM)] + [hbm] * 5,
        out_specs=pl.BlockSpec(memory_space=pltpu.VMEM),
        scratch_shapes=[
            pltpu.VMEM((tokens, width), BF16),
            pltpu.VMEM((tokens, width), BF16),
            pltpu.VMEM((rank, width), BF16),
            pltpu.VMEM((rank, width), BF16),
            pltpu.VMEM((rank, rank), F32),
            pltpu.VMEM((rank, rank), F32),
            pltpu.VMEM((count, rank * rank), BF16),
            pltpu.VMEM((2 * pair, 2 * pair), BF16),
            pltpu.VMEM((half, pair), BF16),
            pltpu.VMEM((n, half, pair), BF16),
            pltpu.VMEM((n * half, pair), F32),
            pltpu.VMEM((m, rows, count), F32),
            pltpu.VMEM((m, rows, count), F32),
            pltpu.SemaphoreType.DMA((4, CHUNKS)),
            pltpu.SemaphoreType.DMA((4,)),
            pltpu.SemaphoreType.DMA((n,)),
            pltpu.SemaphoreType.DMA((n,)),
            pltpu.SemaphoreType.DMA((m,)),
            pltpu.SemaphoreType.DMA((m,)),
        ],
        compiler_params=pltpu.CompilerParams(
            collective_id=0, has_side_effects=True, vmem_limit_bytes=55212 * 1024
        ),
    )(*args)


def solution(mesh):
    n, m = mesh.shape["dp"], mesh.shape["layer"]
    in_specs = (
        P("layer", "dp", None, None),
        P("layer", "dp", None, None),
        P("dp"),
        P("layer", None, None),
        P("layer", None, None),
        P("layer", None, None),
        P("layer", None, None),
        P("layer", "dp", None),
    )
    return jax.shard_map(
        functools.partial(body, n, m),
        mesh=mesh,
        in_specs=in_specs,
        out_specs=P("layer", "dp"),
        check_vma=False,
    )
```

```python
import functools

import jax
import jax.numpy as jnp
from jax import lax
from jax.experimental import pallas as pl
from jax.experimental.pallas import tpu as pltpu
from jax.sharding import PartitionSpec as P

MESH = pl.DeviceIdType.MESH
F32 = jnp.float32
BF16 = jnp.bfloat16
NT = (((1,), (1,)), ((), ()))
CHUNKS = 1


def split(x):
    high = x.astype(BF16).astype(F32)
    return high, x - high


def dot_nt(a, b):
    return lax.dot_general(a, b, NT, preferred_element_type=F32)


def kernel(
    n,
    m,
    inputs_hbm,
    cotangents_hbm,
    length,
    proj_in_hbm,
    proj_out_hbm,
    out_factor_hbm,
    in_factor_hbm,
    train_hbm,
    out_ref,
    inputs,
    cotangents,
    proj_in,
    proj_out,
    out_factor,
    in_factor,
    train,
    weights,
    own,
    gathered,
    wide,
    partial,
    arrived,
    load_sem,
    small_sem,
    send_sem,
    recv_sem,
    layer_send_sem,
    layer_recv_sem,
):
    me = lax.axis_index("dp")
    layer = lax.axis_index("layer")
    tokens, width = inputs.shape
    rank = proj_in.shape[0]
    step = width // CHUNKS

    def load(sem, src, dst):
        copy = pltpu.make_async_copy(src, dst, sem)
        copy.start()
        return copy

    def columns(c):
        return pl.ds(c * step, step)

    out_loads = []
    in_loads = []
    for c in range(CHUNKS):
        out_loads.append(
            (
                load(load_sem.at[0, c], proj_out_hbm.at[0, :, columns(c)], proj_out.at[:, columns(c)]),
                load(load_sem.at[1, c], cotangents_hbm.at[0, 0, :, columns(c)], cotangents.at[:, columns(c)]),
            )
        )
    out_factor_load = load(small_sem.at[0], out_factor_hbm.at[0], out_factor)
    in_factor_load = load(small_sem.at[1], in_factor_hbm.at[0], in_factor)
    for c in range(CHUNKS):
        in_loads.append(
            (
                load(load_sem.at[2, c], proj_in_hbm.at[0, :, columns(c)], proj_in.at[:, columns(c)]),
                load(load_sem.at[3, c], inputs_hbm.at[0, 0, :, columns(c)], inputs.at[:, columns(c)]),
            )
        )
    train_load = load(small_sem.at[3], train_hbm.at[0], train)

    barrier = pltpu.get_barrier_semaphore()
    core = lax.rem(me, 2)
    sibling = me + 1 - 2 * core
    peers = [lax.rem(me + 2 * k, n) for k in range(1, n // 2)]
    layers = [lax.rem(layer + k, m) for k in range(1, m)]
    greeted = [(peer, layer) for peer in peers + [sibling]] + [(me, other) for other in layers]
    for device in greeted:
        pl.semaphore_signal(barrier, inc=1, device_id=device, device_id_type=MESH)

    out_factor_load.wait()
    in_factor_load.wait()
    half = rank // 2
    pair = 2 * rank
    factor_rows = jnp.concatenate(
        [out_factor[pl.ds(0, half, stride=2), :], out_factor[pl.ds(1, half, stride=2), :]], axis=1
    )
    left = jnp.concatenate(split(factor_rows), axis=1).astype(BF16)
    in_high, in_low = split(in_factor[...])
    none = jnp.zeros((rank, rank), F32)
    top = jnp.concatenate([in_high, none, in_low, none], axis=1)
    bottom = jnp.concatenate([none, in_high, none, in_low], axis=1)
    weights[...] = jnp.concatenate([top, bottom, top, bottom], axis=0).astype(BF16)

    def project(loads, proj, values):
        total = None
        for c in range(CHUNKS):
            for copy in loads[c]:
                copy.wait()
            term = dot_nt(proj[:, columns(c)], values[:, columns(c)])
            total = term if total is None else total + term
        return total

    out_side = project(out_loads, proj_out, cotangents)
    slots = lax.broadcasted_iota(jnp.int32, (rank, tokens), 1)
    out_side = jnp.where(slots < length[0], out_side, 0.0)
    pl.semaphore_wait(barrier, len(greeted))
    in_side = project(in_loads, proj_in, inputs)
    out_twice = jnp.concatenate([out_side, out_side], axis=0).astype(BF16)
    in_twice = jnp.concatenate([in_side, in_side], axis=0).astype(BF16)
    grads = dot_nt(out_twice, in_twice)
    rows = lax.broadcasted_iota(jnp.int32, (pair, pair), 0) < rank
    cols = lax.broadcasted_iota(jnp.int32, (pair, pair), 1) < rank
    grads = jnp.where(rows == cols, grads, 0.0).astype(BF16)
    projected = jnp.dot(left, jnp.concatenate([grads, grads], axis=0), preferred_element_type=F32)
    projected = jnp.concatenate(split(projected), axis=1).astype(BF16)
    both = jnp.dot(projected, weights[...], preferred_element_type=F32)
    own[...] = (both[:, :pair] + both[:, pair:]).astype(BF16)

    sends = []

    def share(block, source, target):
        copy = pltpu.make_async_remote_copy(
            src_ref=block,
            dst_ref=gathered.at[source],
            send_sem=send_sem.at[len(sends)],
            recv_sem=recv_sem.at[source],
            device_id=(target, layer),
            device_id_type=MESH,
        )
        copy.start()
        sends.append(copy)

    def arrive(source):
        pltpu.make_async_remote_copy(
            src_ref=own,
            dst_ref=gathered.at[source],
            send_sem=send_sem.at[0],
            recv_sem=recv_sem.at[source],
            device_id=(sibling, layer),
            device_id_type=MESH,
        ).wait_recv()

    for peer in peers:
        share(own, me, peer)
    share(own, me, sibling)
    gathered[me] = own[...]
    for peer in peers:
        arrive(peer)
        share(gathered.at[peer], peer, sibling)
    train_load.wait()
    arrive(sibling)
    for k in range(1, n // 2):
        arrive(lax.rem(sibling + 2 * k, n))

    wide[...] = gathered[...].astype(F32).reshape(wide.shape)
    conditioned = jnp.concatenate(
        [wide[pl.ds(j, n, stride=half), :] for j in range(half)], axis=1
    ).astype(BF16)
    scores = dot_nt(conditioned, train[...])
    partial[...] = scores.reshape(partial.shape)
    layer_sends = []
    for k in range(1, m):
        copy = pltpu.make_async_remote_copy(
            src_ref=partial.at[layers[k - 1]],
            dst_ref=arrived.at[k],
            send_sem=layer_send_sem.at[k],
            recv_sem=layer_recv_sem.at[k],
            device_id=(me, layers[k - 1]),
            device_id_type=MESH,
        )
        copy.start()
        layer_sends.append(copy)
    total = partial[layer]
    for copy in sends:
        copy.wait_send()
    for k in range(1, m):
        layer_sends[k - 1].wait_recv()
        total = total + arrived[k]
    out_ref[...] = total
    for copy in layer_sends:
        copy.wait_send()


def body(n, m, *args):
    inputs, _, _, proj_in, _, _, _, train = args
    _, _, tokens, width = inputs.shape
    rank = proj_in.shape[1]
    count = train.shape[1]
    rows = n // m
    half, pair = rank // 2, 2 * rank
    hbm = pl.BlockSpec(memory_space=pltpu.HBM)
    return pl.pallas_call(
        functools.partial(kernel, n, m),
        out_shape=jax.ShapeDtypeStruct((rows, count), F32),
        in_specs=[hbm, hbm, pl.BlockSpec(memory_space=pltpu.SMEM)] + [hbm] * 5,
        out_specs=pl.BlockSpec(memory_space=pltpu.VMEM),
        scratch_shapes=[
            pltpu.VMEM((tokens, width), BF16),
            pltpu.VMEM((tokens, width), BF16),
            pltpu.VMEM((rank, width), BF16),
            pltpu.VMEM((rank, width), BF16),
            pltpu.VMEM((rank, rank), F32),
            pltpu.VMEM((rank, rank), F32),
            pltpu.VMEM((count, rank * rank), BF16),
            pltpu.VMEM((2 * pair, 2 * pair), BF16),
            pltpu.VMEM((half, pair), BF16),
            pltpu.VMEM((n, half, pair), BF16),
            pltpu.VMEM((n * half, pair), F32),
            pltpu.VMEM((m, rows, count), F32),
            pltpu.VMEM((m, rows, count), F32),
            pltpu.SemaphoreType.DMA((4, CHUNKS)),
            pltpu.SemaphoreType.DMA((4,)),
            pltpu.SemaphoreType.DMA((n,)),
            pltpu.SemaphoreType.DMA((n,)),
            pltpu.SemaphoreType.DMA((m,)),
            pltpu.SemaphoreType.DMA((m,)),
        ],
        compiler_params=pltpu.CompilerParams(
            collective_id=0, has_side_effects=True, vmem_limit_bytes=55212 * 1024
        ),
    )(*args)


def solution(mesh):
    n, m = mesh.shape["dp"], mesh.shape["layer"]
    in_specs = (
        P("layer", "dp", None, None),
        P("layer", "dp", None, None),
        P("dp"),
        P("layer", None, None),
        P("layer", None, None),
        P("layer", None, None),
        P("layer", None, None),
        P("layer", "dp", None),
    )
    return jax.shard_map(
        functools.partial(body, n, m),
        mesh=mesh,
        in_specs=in_specs,
        out_specs=P("layer", "dp"),
        check_vma=False,
    )
```

```python
import functools

import jax
import jax.numpy as jnp
from jax import lax
from jax.experimental import pallas as pl
from jax.experimental.pallas import tpu as pltpu
from jax.sharding import PartitionSpec as P

MESH = pl.DeviceIdType.MESH
F32 = jnp.float32
BF16 = jnp.bfloat16
NT = (((1,), (1,)), ((), ()))
CHUNKS = 1


def split(x):
    high = x.astype(BF16).astype(F32)
    return high, x - high


def dot_nt(a, b):
    return lax.dot_general(a, b, NT, preferred_element_type=F32)


def kernel(
    n,
    m,
    inputs_hbm,
    cotangents_hbm,
    length,
    proj_in_hbm,
    proj_out_hbm,
    out_factor_hbm,
    in_factor_hbm,
    train_hbm,
    out_ref,
    inputs,
    cotangents,
    proj_in,
    proj_out,
    out_factor,
    in_factor,
    train,
    weights,
    own,
    gathered,
    wide,
    partial,
    arrived,
    load_sem,
    small_sem,
    send_sem,
    recv_sem,
    layer_send_sem,
    layer_recv_sem,
):
    me = lax.axis_index("dp")
    layer = lax.axis_index("layer")
    tokens, width = inputs.shape
    rank = proj_in.shape[0]
    step = width // CHUNKS

    def load(sem, src, dst):
        copy = pltpu.make_async_copy(src, dst, sem)
        copy.start()
        return copy

    def columns(c):
        return pl.ds(c * step, step)

    out_factor_load = load(small_sem.at[0], out_factor_hbm.at[0], out_factor)
    in_factor_load = load(small_sem.at[1], in_factor_hbm.at[0], in_factor)
    out_loads = []
    in_loads = []
    for c in range(CHUNKS):
        out_loads.append(
            (
                load(load_sem.at[0, c], proj_out_hbm.at[0, :, columns(c)], proj_out.at[:, columns(c)]),
                load(load_sem.at[1, c], cotangents_hbm.at[0, 0, :, columns(c)], cotangents.at[:, columns(c)]),
            )
        )
    for c in range(CHUNKS):
        in_loads.append(
            (
                load(load_sem.at[2, c], proj_in_hbm.at[0, :, columns(c)], proj_in.at[:, columns(c)]),
                load(load_sem.at[3, c], inputs_hbm.at[0, 0, :, columns(c)], inputs.at[:, columns(c)]),
            )
        )

    barrier = pltpu.get_barrier_semaphore()
    core = lax.rem(me, 2)
    sibling = me + 1 - 2 * core
    peers = [lax.rem(me + 2 * k, n) for k in range(1, n // 2)]
    layers = [lax.rem(layer + k, m) for k in range(1, m)]
    greeted = [(peer, layer) for peer in peers + [sibling]] + [(me, other) for other in layers]
    for device in greeted:
        pl.semaphore_signal(barrier, inc=1, device_id=device, device_id_type=MESH)

    out_factor_load.wait()
    in_factor_load.wait()
    half = rank // 2
    pair = 2 * rank
    factor_rows = jnp.concatenate(
        [out_factor[pl.ds(0, half, stride=2), :], out_factor[pl.ds(1, half, stride=2), :]], axis=1
    )
    left = jnp.concatenate(split(factor_rows), axis=1).astype(BF16)
    in_high, in_low = split(in_factor[...])
    none = jnp.zeros((rank, rank), F32)
    top = jnp.concatenate([in_high, none, in_low, none], axis=1)
    bottom = jnp.concatenate([none, in_high, none, in_low], axis=1)
    weights[...] = jnp.concatenate([top, bottom, top, bottom], axis=0).astype(BF16)

    def project(loads, proj, values):
        total = None
        for c in range(CHUNKS):
            for copy in loads[c]:
                copy.wait()
            term = dot_nt(values[:, columns(c)], proj[:, columns(c)])
            total = term if total is None else total + term
        return total

    out_side = project(out_loads, proj_out, cotangents)
    train_load = load(small_sem.at[3], train_hbm.at[0], train)
    slots = lax.broadcasted_iota(jnp.int32, (tokens, rank), 0)
    out_side = jnp.where(slots < length[0], out_side, 0.0).T
    out_twice = jnp.concatenate([out_side, out_side], axis=0).astype(BF16)
    pl.semaphore_wait(barrier, len(greeted))
    in_side = project(in_loads, proj_in, inputs)
    in_twice = jnp.concatenate([in_side, in_side], axis=1).astype(BF16)
    grads = jnp.dot(out_twice, in_twice, preferred_element_type=F32)
    rows = lax.broadcasted_iota(jnp.int32, (pair, pair), 0) < rank
    cols = lax.broadcasted_iota(jnp.int32, (pair, pair), 1) < rank
    grads = jnp.where(rows == cols, grads, 0.0).astype(BF16)
    projected = jnp.dot(left, jnp.concatenate([grads, grads], axis=0), preferred_element_type=F32)
    projected = jnp.concatenate(split(projected), axis=1).astype(BF16)
    both = jnp.dot(projected, weights[...], preferred_element_type=F32)
    own[...] = (both[:, :pair] + both[:, pair:]).astype(BF16)

    sends = []

    def share(block, source, target):
        copy = pltpu.make_async_remote_copy(
            src_ref=block,
            dst_ref=gathered.at[source],
            send_sem=send_sem.at[len(sends)],
            recv_sem=recv_sem.at[source],
            device_id=(target, layer),
            device_id_type=MESH,
        )
        copy.start()
        sends.append(copy)

    def widen(block, source):
        wide[pl.ds(pl.multiple_of(source * half, half), half), :] = block[...].astype(F32)

    def arrive(source):
        pltpu.make_async_remote_copy(
            src_ref=own,
            dst_ref=gathered.at[source],
            send_sem=send_sem.at[0],
            recv_sem=recv_sem.at[source],
            device_id=(sibling, layer),
            device_id_type=MESH,
        ).wait_recv()

    for peer in peers:
        share(own, me, peer)
    share(own, me, sibling)
    widen(own, me)
    for peer in peers:
        arrive(peer)
        share(gathered.at[peer], peer, sibling)
        widen(gathered.at[peer], peer)
    train_load.wait()
    for k in range(n // 2):
        source = lax.rem(sibling + 2 * k, n)
        arrive(source)
        widen(gathered.at[source], source)

    conditioned = jnp.concatenate(
        [wide[pl.ds(j, n, stride=half), :] for j in range(half)], axis=1
    ).astype(BF16)
    scores = dot_nt(train[...], conditioned).T
    partial[...] = scores.reshape(partial.shape)
    layer_sends = []
    for k in range(1, m):
        copy = pltpu.make_async_remote_copy(
            src_ref=partial.at[layers[k - 1]],
            dst_ref=arrived.at[k],
            send_sem=layer_send_sem.at[k],
            recv_sem=layer_recv_sem.at[k],
            device_id=(me, layers[k - 1]),
            device_id_type=MESH,
        )
        copy.start()
        layer_sends.append(copy)
    total = partial[layer]
    for copy in sends:
        copy.wait_send()
    for k in range(1, m):
        layer_sends[k - 1].wait_recv()
        total = total + arrived[k]
    out_ref[...] = total
    for copy in layer_sends:
        copy.wait_send()


def body(n, m, *args):
    inputs, _, _, proj_in, _, _, _, train = args
    _, _, tokens, width = inputs.shape
    rank = proj_in.shape[1]
    count = train.shape[1]
    rows = n // m
    half, pair = rank // 2, 2 * rank
    hbm = pl.BlockSpec(memory_space=pltpu.HBM)
    return pl.pallas_call(
        functools.partial(kernel, n, m),
        out_shape=jax.ShapeDtypeStruct((rows, count), F32),
        in_specs=[hbm, hbm, pl.BlockSpec(memory_space=pltpu.SMEM)] + [hbm] * 5,
        out_specs=pl.BlockSpec(memory_space=pltpu.VMEM),
        scratch_shapes=[
            pltpu.VMEM((tokens, width), BF16),
            pltpu.VMEM((tokens, width), BF16),
            pltpu.VMEM((rank, width), BF16),
            pltpu.VMEM((rank, width), BF16),
            pltpu.VMEM((rank, rank), F32),
            pltpu.VMEM((rank, rank), F32),
            pltpu.VMEM((count, rank * rank), BF16),
            pltpu.VMEM((2 * pair, 2 * pair), BF16),
            pltpu.VMEM((half, pair), BF16),
            pltpu.VMEM((n, half, pair), BF16),
            pltpu.VMEM((n * half, pair), F32),
            pltpu.VMEM((m, rows, count), F32),
            pltpu.VMEM((m, rows, count), F32),
            pltpu.SemaphoreType.DMA((4, CHUNKS)),
            pltpu.SemaphoreType.DMA((4,)),
            pltpu.SemaphoreType.DMA((n,)),
            pltpu.SemaphoreType.DMA((n,)),
            pltpu.SemaphoreType.DMA((m,)),
            pltpu.SemaphoreType.DMA((m,)),
        ],
        compiler_params=pltpu.CompilerParams(
            collective_id=0, has_side_effects=True, vmem_limit_bytes=55212 * 1024
        ),
    )(*args)


def solution(mesh):
    n, m = mesh.shape["dp"], mesh.shape["layer"]
    in_specs = (
        P("layer", "dp", None, None),
        P("layer", "dp", None, None),
        P("dp"),
        P("layer", None, None),
        P("layer", None, None),
        P("layer", None, None),
        P("layer", None, None),
        P("layer", "dp", None),
    )
    return jax.shard_map(
        functools.partial(body, n, m),
        mesh=mesh,
        in_specs=in_specs,
        out_specs=P("layer", "dp"),
        check_vma=False,
    )
```

```python
import functools

import jax
import jax.numpy as jnp
from jax import lax
from jax.experimental import pallas as pl
from jax.experimental.pallas import tpu as pltpu
from jax.sharding import PartitionSpec as P

MESH = pl.DeviceIdType.MESH
F32 = jnp.float32
BF16 = jnp.bfloat16
NT = (((1,), (1,)), ((), ()))
CHUNKS = 1


def split(x):
    high = x.astype(BF16).astype(F32)
    return high, x - high


def dot_nt(a, b):
    return lax.dot_general(a, b, NT, preferred_element_type=F32)


def kernel(
    n,
    m,
    inputs_hbm,
    cotangents_hbm,
    length,
    proj_in_hbm,
    proj_out_hbm,
    out_factor_hbm,
    in_factor_hbm,
    train_hbm,
    out_ref,
    inputs,
    cotangents,
    proj_in,
    proj_out,
    out_factor,
    in_factor,
    train,
    weights,
    own,
    gathered,
    wide,
    partial,
    arrived,
    load_sem,
    small_sem,
    send_sem,
    recv_sem,
    layer_send_sem,
    layer_recv_sem,
):
    me = lax.axis_index("dp")
    layer = lax.axis_index("layer")
    tokens, width = inputs.shape
    rank = proj_in.shape[0]
    step = width // CHUNKS

    def load(sem, src, dst):
        copy = pltpu.make_async_copy(src, dst, sem)
        copy.start()
        return copy

    def columns(c):
        return pl.ds(c * step, step)

    out_loads = []
    for c in range(CHUNKS):
        out_loads.append(
            (
                load(load_sem.at[0, c], proj_out_hbm.at[0, :, columns(c)], proj_out.at[:, columns(c)]),
                load(load_sem.at[1, c], cotangents_hbm.at[0, 0, :, columns(c)], cotangents.at[:, columns(c)]),
            )
        )
    barrier = pltpu.get_barrier_semaphore()
    core = lax.rem(me, 2)
    sibling = me + 1 - 2 * core
    peers = [lax.rem(me + 2 * k, n) for k in range(1, n // 2)]
    layers = [lax.rem(layer + k, m) for k in range(1, m)]
    greeted = [(peer, layer) for peer in peers + [sibling]] + [(me, other) for other in layers]
    for device in greeted:
        pl.semaphore_signal(barrier, inc=1, device_id=device, device_id_type=MESH)

    out_factor_load = load(small_sem.at[0], out_factor_hbm.at[0], out_factor)
    in_factor_load = load(small_sem.at[1], in_factor_hbm.at[0], in_factor)
    in_loads = []
    for c in range(CHUNKS):
        in_loads.append(
            (
                load(load_sem.at[2, c], proj_in_hbm.at[0, :, columns(c)], proj_in.at[:, columns(c)]),
                load(load_sem.at[3, c], inputs_hbm.at[0, 0, :, columns(c)], inputs.at[:, columns(c)]),
            )
        )

    out_factor_load.wait()
    in_factor_load.wait()
    half = rank // 2
    pair = 2 * rank
    factor_rows = jnp.concatenate(
        [out_factor[pl.ds(0, half, stride=2), :], out_factor[pl.ds(1, half, stride=2), :]], axis=1
    )
    left = jnp.concatenate(split(factor_rows), axis=1).astype(BF16)
    in_high, in_low = split(in_factor[...])
    none = jnp.zeros((rank, rank), F32)
    top = jnp.concatenate([in_high, none, in_low, none], axis=1)
    bottom = jnp.concatenate([none, in_high, none, in_low], axis=1)
    weights[...] = jnp.concatenate([top, bottom, top, bottom], axis=0).astype(BF16)

    def project(loads, proj, values):
        total = None
        for c in range(CHUNKS):
            for copy in loads[c]:
                copy.wait()
            term = dot_nt(values[:, columns(c)], proj[:, columns(c)])
            total = term if total is None else total + term
        return total

    out_side = project(out_loads, proj_out, cotangents)
    train_load = load(small_sem.at[3], train_hbm.at[0], train)
    slots = lax.broadcasted_iota(jnp.int32, (tokens, rank), 0)
    out_side = jnp.where(slots < length[0], out_side, 0.0).T
    out_twice = jnp.concatenate([out_side, out_side], axis=0).astype(BF16)
    in_side = project(in_loads, proj_in, inputs)
    in_twice = jnp.concatenate([in_side, in_side], axis=1).astype(BF16)
    grads = jnp.dot(out_twice, in_twice, preferred_element_type=F32)
    rows = lax.broadcasted_iota(jnp.int32, (pair, pair), 0) < rank
    cols = lax.broadcasted_iota(jnp.int32, (pair, pair), 1) < rank
    grads = jnp.where(rows == cols, grads, 0.0).astype(BF16)
    projected = jnp.dot(left, jnp.concatenate([grads, grads], axis=0), preferred_element_type=F32)
    projected = jnp.concatenate(split(projected), axis=1).astype(BF16)
    both = jnp.dot(projected, weights[...], preferred_element_type=F32)
    own[...] = (both[:, :pair] + both[:, pair:]).astype(BF16)

    pl.semaphore_wait(barrier, len(greeted))
    sends = []

    def share(block, source, target):
        copy = pltpu.make_async_remote_copy(
            src_ref=block,
            dst_ref=gathered.at[source],
            send_sem=send_sem.at[len(sends)],
            recv_sem=recv_sem.at[source],
            device_id=(target, layer),
            device_id_type=MESH,
        )
        copy.start()
        sends.append(copy)

    def widen(block, source):
        wide[pl.ds(pl.multiple_of(source * half, half), half), :] = block[...].astype(F32)

    def arrive(source):
        pltpu.make_async_remote_copy(
            src_ref=own,
            dst_ref=gathered.at[source],
            send_sem=send_sem.at[0],
            recv_sem=recv_sem.at[source],
            device_id=(sibling, layer),
            device_id_type=MESH,
        ).wait_recv()

    for peer in peers:
        share(own, me, peer)
    share(own, me, sibling)
    widen(own, me)
    for peer in peers:
        arrive(peer)
        share(gathered.at[peer], peer, sibling)
        widen(gathered.at[peer], peer)
    train_load.wait()
    for k in range(n // 2):
        source = lax.rem(sibling + 2 * k, n)
        arrive(source)
        widen(gathered.at[source], source)

    conditioned = jnp.concatenate(
        [wide[pl.ds(j, n, stride=half), :] for j in range(half)], axis=1
    ).astype(BF16)
    scores = dot_nt(train[...], conditioned).T
    partial[...] = scores.reshape(partial.shape)
    layer_sends = []
    for k in range(1, m):
        copy = pltpu.make_async_remote_copy(
            src_ref=partial.at[layers[k - 1]],
            dst_ref=arrived.at[k],
            send_sem=layer_send_sem.at[k],
            recv_sem=layer_recv_sem.at[k],
            device_id=(me, layers[k - 1]),
            device_id_type=MESH,
        )
        copy.start()
        layer_sends.append(copy)
    total = partial[layer]
    for copy in sends:
        copy.wait_send()
    for k in range(1, m):
        layer_sends[k - 1].wait_recv()
        total = total + arrived[k]
    out_ref[...] = total
    for copy in layer_sends:
        copy.wait_send()


def body(n, m, *args):
    inputs, _, _, proj_in, _, _, _, train = args
    _, _, tokens, width = inputs.shape
    rank = proj_in.shape[1]
    count = train.shape[1]
    rows = n // m
    half, pair = rank // 2, 2 * rank
    hbm = pl.BlockSpec(memory_space=pltpu.HBM)
    return pl.pallas_call(
        functools.partial(kernel, n, m),
        out_shape=jax.ShapeDtypeStruct((rows, count), F32),
        in_specs=[hbm, hbm, pl.BlockSpec(memory_space=pltpu.SMEM)] + [hbm] * 5,
        out_specs=pl.BlockSpec(memory_space=pltpu.VMEM),
        scratch_shapes=[
            pltpu.VMEM((tokens, width), BF16),
            pltpu.VMEM((tokens, width), BF16),
            pltpu.VMEM((rank, width), BF16),
            pltpu.VMEM((rank, width), BF16),
            pltpu.VMEM((rank, rank), F32),
            pltpu.VMEM((rank, rank), F32),
            pltpu.VMEM((count, rank * rank), BF16),
            pltpu.VMEM((2 * pair, 2 * pair), BF16),
            pltpu.VMEM((half, pair), BF16),
            pltpu.VMEM((n, half, pair), BF16),
            pltpu.VMEM((n * half, pair), F32),
            pltpu.VMEM((m, rows, count), F32),
            pltpu.VMEM((m, rows, count), F32),
            pltpu.SemaphoreType.DMA((4, CHUNKS)),
            pltpu.SemaphoreType.DMA((4,)),
            pltpu.SemaphoreType.DMA((n,)),
            pltpu.SemaphoreType.DMA((n,)),
            pltpu.SemaphoreType.DMA((m,)),
            pltpu.SemaphoreType.DMA((m,)),
        ],
        compiler_params=pltpu.CompilerParams(
            collective_id=0, has_side_effects=True, vmem_limit_bytes=55212 * 1024
        ),
    )(*args)


def solution(mesh):
    n, m = mesh.shape["dp"], mesh.shape["layer"]
    in_specs = (
        P("layer", "dp", None, None),
        P("layer", "dp", None, None),
        P("dp"),
        P("layer", None, None),
        P("layer", None, None),
        P("layer", None, None),
        P("layer", None, None),
        P("layer", "dp", None),
    )
    return jax.shard_map(
        functools.partial(body, n, m),
        mesh=mesh,
        in_specs=in_specs,
        out_specs=P("layer", "dp"),
        check_vma=False,
    )
```

```python
import functools

import jax
import jax.numpy as jnp
from jax import lax
from jax.experimental import pallas as pl
from jax.experimental.pallas import tpu as pltpu
from jax.sharding import PartitionSpec as P

MESH = pl.DeviceIdType.MESH
F32 = jnp.float32
BF16 = jnp.bfloat16
NT = (((1,), (1,)), ((), ()))
CHUNKS = 1
STRIPS = 4


def split(x):
    high = x.astype(BF16).astype(F32)
    return high, x - high


def dot_nt(a, b):
    return lax.dot_general(a, b, NT, preferred_element_type=F32)


def kernel(
    n,
    m,
    inputs_hbm,
    cotangents_hbm,
    length,
    proj_in_hbm,
    proj_out_hbm,
    out_factor_hbm,
    in_factor_hbm,
    train_hbm,
    out_ref,
    inputs,
    cotangents,
    proj_in,
    proj_out,
    out_factor,
    in_factor,
    train,
    weights,
    own,
    gathered,
    wide,
    partial,
    arrived,
    load_sem,
    small_sem,
    train_sem,
    send_sem,
    recv_sem,
    layer_send_sem,
    layer_recv_sem,
):
    me = lax.axis_index("dp")
    layer = lax.axis_index("layer")
    tokens, width = inputs.shape
    rank = proj_in.shape[0]
    step = width // CHUNKS

    def load(sem, src, dst):
        copy = pltpu.make_async_copy(src, dst, sem)
        copy.start()
        return copy

    def columns(c):
        return pl.ds(c * step, step)

    out_loads = []
    for c in range(CHUNKS):
        out_loads.append(
            (
                load(load_sem.at[0, c], proj_out_hbm.at[0, :, columns(c)], proj_out.at[:, columns(c)]),
                load(load_sem.at[1, c], cotangents_hbm.at[0, 0, :, columns(c)], cotangents.at[:, columns(c)]),
            )
        )
    barrier = pltpu.get_barrier_semaphore()
    core = lax.rem(me, 2)
    sibling = me + 1 - 2 * core
    peers = [lax.rem(me + 2 * k, n) for k in range(1, n // 2)]
    layers = [lax.rem(layer + k, m) for k in range(1, m)]
    partners = [(sibling, layer)] + [(dp, other) for other in layers for dp in (me, sibling)]
    greeted = [(peer, layer) for peer in peers] + partners
    for device in greeted:
        pl.semaphore_signal(barrier, inc=1, device_id=device, device_id_type=MESH)

    out_factor_load = load(small_sem.at[0], out_factor_hbm.at[0], out_factor)
    in_factor_load = load(small_sem.at[1], in_factor_hbm.at[0], in_factor)
    in_loads = []
    for c in range(CHUNKS):
        in_loads.append(
            (
                load(load_sem.at[2, c], proj_in_hbm.at[0, :, columns(c)], proj_in.at[:, columns(c)]),
                load(load_sem.at[3, c], inputs_hbm.at[0, 0, :, columns(c)], inputs.at[:, columns(c)]),
            )
        )

    out_factor_load.wait()
    in_factor_load.wait()
    half = rank // 2
    pair = 2 * rank
    factor_rows = jnp.concatenate(
        [out_factor[pl.ds(0, half, stride=2), :], out_factor[pl.ds(1, half, stride=2), :]], axis=1
    )
    left = jnp.concatenate(split(factor_rows), axis=1).astype(BF16)
    in_high, in_low = split(in_factor[...])
    none = jnp.zeros((rank, rank), F32)
    top = jnp.concatenate([in_high, none, in_low, none], axis=1)
    bottom = jnp.concatenate([none, in_high, none, in_low], axis=1)
    weights[...] = jnp.concatenate([top, bottom, top, bottom], axis=0).astype(BF16)

    def project(loads, proj, values):
        total = None
        for c in range(CHUNKS):
            for copy in loads[c]:
                copy.wait()
            term = dot_nt(values[:, columns(c)], proj[:, columns(c)])
            total = term if total is None else total + term
        return total

    out_side = project(out_loads, proj_out, cotangents)
    slots = lax.broadcasted_iota(jnp.int32, (tokens, rank), 0)
    out_side = jnp.where(slots < length[0], out_side, 0.0).T
    out_twice = jnp.concatenate([out_side, out_side], axis=0).astype(BF16)
    pl.semaphore_wait(barrier, len(greeted))
    train_shares = []
    strip = train.shape[1] // STRIPS
    for c in range(STRIPS):
        copy = pltpu.make_async_remote_copy(
            src_ref=train_hbm.at[0, pl.ds(c * strip, strip), :],
            dst_ref=train.at[core, pl.ds(c * strip, strip), :],
            send_sem=train_sem.at[0, c],
            recv_sem=train_sem.at[1, c],
            device_id=(sibling, layer),
            device_id_type=MESH,
        )
        copy.start()
        train_shares.append(copy)
    train_load = load(small_sem.at[2], train_hbm.at[0], train.at[core])
    in_side = project(in_loads, proj_in, inputs)
    in_twice = jnp.concatenate([in_side, in_side], axis=1).astype(BF16)
    grads = jnp.dot(out_twice, in_twice, preferred_element_type=F32)
    rows = lax.broadcasted_iota(jnp.int32, (pair, pair), 0) < rank
    cols = lax.broadcasted_iota(jnp.int32, (pair, pair), 1) < rank
    grads = jnp.where(rows == cols, grads, 0.0).astype(BF16)
    projected = jnp.dot(left, jnp.concatenate([grads, grads], axis=0), preferred_element_type=F32)
    projected = jnp.concatenate(split(projected), axis=1).astype(BF16)
    both = jnp.dot(projected, weights[...], preferred_element_type=F32)
    own[...] = (both[:, :pair] + both[:, pair:]).astype(BF16)

    place = me // 2
    sends = []
    for k, peer in enumerate(peers):
        copy = pltpu.make_async_remote_copy(
            src_ref=own,
            dst_ref=gathered.at[place],
            send_sem=send_sem.at[k],
            recv_sem=recv_sem.at[place],
            device_id=(peer, layer),
            device_id_type=MESH,
        )
        copy.start()
        sends.append(copy)

    def widen(block, index):
        wide[pl.ds(pl.multiple_of(index * half, half), half), :] = block[...].astype(F32)

    widen(own, place)
    train_load.wait()
    for copy in train_shares:
        copy.wait_recv()
    for k, peer in enumerate(peers):
        source = peer // 2
        pltpu.make_async_remote_copy(
            src_ref=own,
            dst_ref=gathered.at[source],
            send_sem=send_sem.at[k],
            recv_sem=recv_sem.at[source],
            device_id=(peer, layer),
            device_id_type=MESH,
        ).wait_recv()
        widen(gathered.at[source], source)
    conditioned = jnp.concatenate(
        [wide[pl.ds(j, n // 2, stride=half), :] for j in range(half)], axis=1
    ).astype(BF16)
    scores = dot_nt(train[...].reshape(2 * train.shape[1], train.shape[2]), conditioned).T
    _, _, rows, count = partial.shape
    for other in range(m):
        for c in range(2):
            partial[other, c] = scores[other * rows : (other + 1) * rows, c * count : (c + 1) * count]
    results = []
    for k, (dp, other) in enumerate(partners):
        copy = pltpu.make_async_remote_copy(
            src_ref=partial.at[other, lax.rem(dp, 2)],
            dst_ref=arrived.at[layer, core],
            send_sem=layer_send_sem.at[k],
            recv_sem=layer_recv_sem.at[layer, core],
            device_id=(dp, other),
            device_id_type=MESH,
        )
        copy.start()
        results.append(copy)
    arrived[layer, core] = partial[layer, core]
    for copy in train_shares:
        copy.wait_send()
    for copy in sends:
        copy.wait_send()
    for k, (dp, other) in enumerate(partners):
        pltpu.make_async_remote_copy(
            src_ref=partial.at[other, lax.rem(dp, 2)],
            dst_ref=arrived.at[other, lax.rem(dp, 2)],
            send_sem=layer_send_sem.at[k],
            recv_sem=layer_recv_sem.at[other, lax.rem(dp, 2)],
            device_id=(dp, other),
            device_id_type=MESH,
        ).wait_recv()
    for c in range(2):
        total = arrived[0, c]
        for other in range(1, m):
            total = total + arrived[other, c]
        out_ref[pl.ds(c, rows, stride=2), :] = total
    for copy in results:
        copy.wait_send()


def body(n, m, *args):
    inputs, _, _, proj_in, _, _, _, train = args
    _, _, tokens, width = inputs.shape
    rank = proj_in.shape[1]
    count = train.shape[1]
    rows = n // m
    half, pair = rank // 2, 2 * rank
    hbm = pl.BlockSpec(memory_space=pltpu.HBM)
    return pl.pallas_call(
        functools.partial(kernel, n, m),
        out_shape=jax.ShapeDtypeStruct((rows, count), F32),
        in_specs=[hbm, hbm, pl.BlockSpec(memory_space=pltpu.SMEM)] + [hbm] * 5,
        out_specs=pl.BlockSpec(memory_space=pltpu.VMEM),
        scratch_shapes=[
            pltpu.VMEM((tokens, width), BF16),
            pltpu.VMEM((tokens, width), BF16),
            pltpu.VMEM((rank, width), BF16),
            pltpu.VMEM((rank, width), BF16),
            pltpu.VMEM((rank, rank), F32),
            pltpu.VMEM((rank, rank), F32),
            pltpu.VMEM((2, count, rank * rank), BF16),
            pltpu.VMEM((2 * pair, 2 * pair), BF16),
            pltpu.VMEM((half, pair), BF16),
            pltpu.VMEM((n // 2, half, pair), BF16),
            pltpu.VMEM((n // 2 * half, pair), F32),
            pltpu.VMEM((m, 2, rows // 2, count), F32),
            pltpu.VMEM((m, 2, rows // 2, count), F32),
            pltpu.SemaphoreType.DMA((4, CHUNKS)),
            pltpu.SemaphoreType.DMA((3,)),
            pltpu.SemaphoreType.DMA((2, STRIPS)),
            pltpu.SemaphoreType.DMA((n // 2,)),
            pltpu.SemaphoreType.DMA((n // 2,)),
            pltpu.SemaphoreType.DMA((2 * m,)),
            pltpu.SemaphoreType.DMA((m, 2)),
        ],
        compiler_params=pltpu.CompilerParams(
            collective_id=0, has_side_effects=True, vmem_limit_bytes=55212 * 1024
        ),
    )(*args)


def solution(mesh):
    n, m = mesh.shape["dp"], mesh.shape["layer"]
    in_specs = (
        P("layer", "dp", None, None),
        P("layer", "dp", None, None),
        P("dp"),
        P("layer", None, None),
        P("layer", None, None),
        P("layer", None, None),
        P("layer", None, None),
        P("layer", "dp", None),
    )
    return jax.shard_map(
        functools.partial(body, n, m),
        mesh=mesh,
        in_specs=in_specs,
        out_specs=P("layer", "dp"),
        check_vma=False,
    )
```

```python
import functools

import jax
import jax.numpy as jnp
from jax import lax
from jax.experimental import pallas as pl
from jax.experimental.pallas import tpu as pltpu
from jax.sharding import PartitionSpec as P

MESH = pl.DeviceIdType.MESH
F32 = jnp.float32
BF16 = jnp.bfloat16
NT = (((1,), (1,)), ((), ()))
CHUNKS = 1


def split(x):
    high = x.astype(BF16).astype(F32)
    return high, x - high


def dot_nt(a, b):
    return lax.dot_general(a, b, NT, preferred_element_type=F32)


def kernel(
    n,
    m,
    inputs_hbm,
    cotangents_hbm,
    length,
    proj_in_hbm,
    proj_out_hbm,
    out_factor_hbm,
    in_factor_hbm,
    train_hbm,
    out_ref,
    inputs,
    cotangents,
    proj_in,
    proj_out,
    out_factor,
    in_factor,
    train,
    weights,
    own,
    gathered,
    wide,
    partial,
    arrived,
    load_sem,
    small_sem,
    send_sem,
    recv_sem,
    layer_send_sem,
    layer_recv_sem,
):
    me = lax.axis_index("dp")
    layer = lax.axis_index("layer")
    tokens, width = inputs.shape
    rank = proj_in.shape[0]
    step = width // CHUNKS

    def load(sem, src, dst):
        copy = pltpu.make_async_copy(src, dst, sem)
        copy.start()
        return copy

    def columns(c):
        return pl.ds(c * step, step)

    out_loads = []
    for c in range(CHUNKS):
        out_loads.append(
            (
                load(load_sem.at[0, c], proj_out_hbm.at[0, :, columns(c)], proj_out.at[:, columns(c)]),
                load(load_sem.at[1, c], cotangents_hbm.at[0, 0, :, columns(c)], cotangents.at[:, columns(c)]),
            )
        )
    barrier = pltpu.get_barrier_semaphore()
    core = lax.rem(me, 2)
    sibling = me + 1 - 2 * core
    peers = [lax.rem(me + 2 * k, n) for k in range(1, n // 2)]
    layers = [lax.rem(layer + k, m) for k in range(1, m)]
    greeted = [(peer, layer) for peer in peers + [sibling]] + [(me, other) for other in layers]
    for device in greeted:
        pl.semaphore_signal(barrier, inc=1, device_id=device, device_id_type=MESH)
    place = me // 2

    @pl.when(place == 0)
    def _():
        for k in range(1, n // 2):
            pl.semaphore_signal(barrier, inc=1, device_id=(sibling + 2 * k, layer), device_id_type=MESH)

    out_factor_load = load(small_sem.at[0], out_factor_hbm.at[0], out_factor)
    in_factor_load = load(small_sem.at[1], in_factor_hbm.at[0], in_factor)
    in_loads = []
    for c in range(CHUNKS):
        in_loads.append(
            (
                load(load_sem.at[2, c], proj_in_hbm.at[0, :, columns(c)], proj_in.at[:, columns(c)]),
                load(load_sem.at[3, c], inputs_hbm.at[0, 0, :, columns(c)], inputs.at[:, columns(c)]),
            )
        )

    out_factor_load.wait()
    in_factor_load.wait()
    half = rank // 2
    pair = 2 * rank
    factor_rows = jnp.concatenate(
        [out_factor[pl.ds(0, half, stride=2), :], out_factor[pl.ds(1, half, stride=2), :]], axis=1
    )
    left = jnp.concatenate(split(factor_rows), axis=1).astype(BF16)
    in_high, in_low = split(in_factor[...])
    none = jnp.zeros((rank, rank), F32)
    top = jnp.concatenate([in_high, none, in_low, none], axis=1)
    bottom = jnp.concatenate([none, in_high, none, in_low], axis=1)
    weights[...] = jnp.concatenate([top, bottom, top, bottom], axis=0).astype(BF16)

    def project(loads, proj, values):
        total = None
        for c in range(CHUNKS):
            for copy in loads[c]:
                copy.wait()
            term = dot_nt(values[:, columns(c)], proj[:, columns(c)])
            total = term if total is None else total + term
        return total

    out_side = project(out_loads, proj_out, cotangents)
    train_load = load(small_sem.at[3], train_hbm.at[0], train)
    slots = lax.broadcasted_iota(jnp.int32, (tokens, rank), 0)
    out_side = jnp.where(slots < length[0], out_side, 0.0).T
    out_twice = jnp.concatenate([out_side, out_side], axis=0).astype(BF16)
    in_side = project(in_loads, proj_in, inputs)
    in_twice = jnp.concatenate([in_side, in_side], axis=1).astype(BF16)
    grads = jnp.dot(out_twice, in_twice, preferred_element_type=F32)
    rows = lax.broadcasted_iota(jnp.int32, (pair, pair), 0) < rank
    cols = lax.broadcasted_iota(jnp.int32, (pair, pair), 1) < rank
    grads = jnp.where(rows == cols, grads, 0.0).astype(BF16)
    projected = jnp.dot(left, jnp.concatenate([grads, grads], axis=0), preferred_element_type=F32)
    projected = jnp.concatenate(split(projected), axis=1).astype(BF16)
    both = jnp.dot(projected, weights[...], preferred_element_type=F32)
    own[...] = (both[:, :pair] + both[:, pair:]).astype(BF16)

    pl.semaphore_wait(barrier, len(greeted) + (place + n // 2 - 1) // (n // 2))
    sends = []

    def share(block, source, target, sem):
        copy = pltpu.make_async_remote_copy(
            src_ref=block,
            dst_ref=gathered.at[source],
            send_sem=send_sem.at[sem],
            recv_sem=recv_sem.at[source],
            device_id=(target, layer),
            device_id_type=MESH,
        )
        copy.start()
        return copy

    def widen(block, source):
        wide[pl.ds(pl.multiple_of(source * half, half), half), :] = block[...].astype(F32)

    def arrive(source):
        pltpu.make_async_remote_copy(
            src_ref=own,
            dst_ref=gathered.at[source],
            send_sem=send_sem.at[0],
            recv_sem=recv_sem.at[source],
            device_id=(sibling, layer),
            device_id_type=MESH,
        ).wait_recv()

    @pl.when(place > 0)
    def _():
        share(own, me, 1 - core, 0)

    for k, peer in enumerate(peers):
        sends.append(share(own, me, peer, 1 + k))
    sends.append(share(own, me, sibling, n // 2))
    widen(own, me)
    for k, peer in enumerate(peers):
        arrive(peer)

        @pl.when(place > 0)
        def _():
            share(gathered.at[peer], peer, sibling, n // 2 + 1 + k)

        widen(gathered.at[peer], peer)
    train_load.wait()
    for k in range(n // 2):
        source = lax.rem(sibling + 2 * k, n)
        arrive(source)
        widen(gathered.at[source], source)

    conditioned = jnp.concatenate(
        [wide[pl.ds(j, n, stride=half), :] for j in range(half)], axis=1
    ).astype(BF16)
    scores = dot_nt(train[...], conditioned).T
    partial[...] = scores.reshape(partial.shape)
    layer_sends = []
    for k in range(1, m):
        copy = pltpu.make_async_remote_copy(
            src_ref=partial.at[layers[k - 1]],
            dst_ref=arrived.at[k],
            send_sem=layer_send_sem.at[k],
            recv_sem=layer_recv_sem.at[k],
            device_id=(me, layers[k - 1]),
            device_id_type=MESH,
        )
        copy.start()
        layer_sends.append(copy)
    total = partial[layer]
    for copy in sends:
        copy.wait_send()

    @pl.when(place > 0)
    def _():
        for sem in [0] + list(range(n // 2 + 1, n)):
            pltpu.make_async_remote_copy(
                src_ref=own,
                dst_ref=gathered.at[me],
                send_sem=send_sem.at[sem],
                recv_sem=recv_sem.at[me],
                device_id=(sibling, layer),
                device_id_type=MESH,
            ).wait_send()

    for k in range(1, m):
        layer_sends[k - 1].wait_recv()
        total = total + arrived[k]
    out_ref[...] = total
    for copy in layer_sends:
        copy.wait_send()


def body(n, m, *args):
    inputs, _, _, proj_in, _, _, _, train = args
    _, _, tokens, width = inputs.shape
    rank = proj_in.shape[1]
    count = train.shape[1]
    rows = n // m
    half, pair = rank // 2, 2 * rank
    hbm = pl.BlockSpec(memory_space=pltpu.HBM)
    return pl.pallas_call(
        functools.partial(kernel, n, m),
        out_shape=jax.ShapeDtypeStruct((rows, count), F32),
        in_specs=[hbm, hbm, pl.BlockSpec(memory_space=pltpu.SMEM)] + [hbm] * 5,
        out_specs=pl.BlockSpec(memory_space=pltpu.VMEM),
        scratch_shapes=[
            pltpu.VMEM((tokens, width), BF16),
            pltpu.VMEM((tokens, width), BF16),
            pltpu.VMEM((rank, width), BF16),
            pltpu.VMEM((rank, width), BF16),
            pltpu.VMEM((rank, rank), F32),
            pltpu.VMEM((rank, rank), F32),
            pltpu.VMEM((count, rank * rank), BF16),
            pltpu.VMEM((2 * pair, 2 * pair), BF16),
            pltpu.VMEM((half, pair), BF16),
            pltpu.VMEM((n, half, pair), BF16),
            pltpu.VMEM((n * half, pair), F32),
            pltpu.VMEM((m, rows, count), F32),
            pltpu.VMEM((m, rows, count), F32),
            pltpu.SemaphoreType.DMA((4, CHUNKS)),
            pltpu.SemaphoreType.DMA((4,)),
            pltpu.SemaphoreType.DMA((n,)),
            pltpu.SemaphoreType.DMA((n,)),
            pltpu.SemaphoreType.DMA((m,)),
            pltpu.SemaphoreType.DMA((m,)),
        ],
        compiler_params=pltpu.CompilerParams(
            collective_id=0, has_side_effects=True, vmem_limit_bytes=55212 * 1024
        ),
    )(*args)


def solution(mesh):
    n, m = mesh.shape["dp"], mesh.shape["layer"]
    in_specs = (
        P("layer", "dp", None, None),
        P("layer", "dp", None, None),
        P("dp"),
        P("layer", None, None),
        P("layer", None, None),
        P("layer", None, None),
        P("layer", None, None),
        P("layer", "dp", None),
    )
    return jax.shard_map(
        functools.partial(body, n, m),
        mesh=mesh,
        in_specs=in_specs,
        out_specs=P("layer", "dp"),
        check_vma=False,
    )
```

```python
import functools

import jax
import jax.numpy as jnp
from jax import lax
from jax.experimental import pallas as pl
from jax.experimental.pallas import tpu as pltpu
from jax.sharding import PartitionSpec as P

MESH = pl.DeviceIdType.MESH
F32 = jnp.float32
BF16 = jnp.bfloat16
NT = (((1,), (1,)), ((), ()))
CHUNKS = 2


def split(x):
    high = x.astype(BF16).astype(F32)
    return high, x - high


def dot_nt(a, b):
    return lax.dot_general(a, b, NT, preferred_element_type=F32)


def kernel(
    n,
    m,
    inputs_hbm,
    cotangents_hbm,
    length,
    proj_in_hbm,
    proj_out_hbm,
    out_factor_hbm,
    in_factor_hbm,
    train_hbm,
    out_ref,
    inputs,
    cotangents,
    proj_in,
    proj_out,
    out_factor,
    in_factor,
    train,
    weights,
    own,
    gathered,
    wide,
    partial,
    arrived,
    load_sem,
    small_sem,
    send_sem,
    recv_sem,
    layer_send_sem,
    layer_recv_sem,
):
    me = lax.axis_index("dp")
    layer = lax.axis_index("layer")
    tokens, width = inputs.shape
    rank = proj_in.shape[0]
    step = width // CHUNKS

    def load(sem, src, dst):
        copy = pltpu.make_async_copy(src, dst, sem)
        copy.start()
        return copy

    def columns(c):
        return pl.ds(c * step, step)

    out_loads = []
    in_loads = []
    for c in range(CHUNKS):
        out_loads.append(
            (
                load(load_sem.at[0, c], proj_out_hbm.at[0, :, columns(c)], proj_out.at[:, columns(c)]),
                load(load_sem.at[1, c], cotangents_hbm.at[0, 0, :, columns(c)], cotangents.at[:, columns(c)]),
            )
        )
    out_factor_load = load(small_sem.at[0], out_factor_hbm.at[0], out_factor)
    in_factor_load = load(small_sem.at[1], in_factor_hbm.at[0], in_factor)
    for c in range(CHUNKS):
        in_loads.append(
            (
                load(load_sem.at[2, c], proj_in_hbm.at[0, :, columns(c)], proj_in.at[:, columns(c)]),
                load(load_sem.at[3, c], inputs_hbm.at[0, 0, :, columns(c)], inputs.at[:, columns(c)]),
            )
        )
    train_load = load(small_sem.at[3], train_hbm.at[0], train)

    barrier = pltpu.get_barrier_semaphore()
    core = lax.rem(me, 2)
    sibling = me + 1 - 2 * core
    peers = [lax.rem(me + 2 * k, n) for k in range(1, n // 2)]
    layers = [lax.rem(layer + k, m) for k in range(1, m)]
    greeted = [(peer, layer) for peer in peers + [sibling]] + [(me, other) for other in layers]
    for device in greeted:
        pl.semaphore_signal(barrier, inc=1, device_id=device, device_id_type=MESH)

    out_factor_load.wait()
    in_factor_load.wait()
    half = rank // 2
    pair = 2 * rank
    factor_rows = jnp.concatenate(
        [out_factor[pl.ds(0, half, stride=2), :], out_factor[pl.ds(1, half, stride=2), :]], axis=1
    )
    left = jnp.concatenate(split(factor_rows), axis=1).astype(BF16)
    in_high, in_low = split(in_factor[...])
    none = jnp.zeros((rank, rank), F32)
    top = jnp.concatenate([in_high, none, in_low, none], axis=1)
    bottom = jnp.concatenate([none, in_high, none, in_low], axis=1)
    weights[...] = jnp.concatenate([top, bottom, top, bottom], axis=0).astype(BF16)

    def project(loads, proj, values):
        total = None
        for c in range(CHUNKS):
            for copy in loads[c]:
                copy.wait()
            term = dot_nt(proj[:, columns(c)], values[:, columns(c)])
            total = term if total is None else total + term
        return total

    out_side = project(out_loads, proj_out, cotangents)
    slots = lax.broadcasted_iota(jnp.int32, (rank, tokens), 1)
    out_side = jnp.where(slots < length[0], out_side, 0.0)
    pl.semaphore_wait(barrier, len(greeted))
    in_side = project(in_loads, proj_in, inputs)
    out_twice = jnp.concatenate([out_side, out_side], axis=0).astype(BF16)
    in_twice = jnp.concatenate([in_side, in_side], axis=0).astype(BF16)
    grads = dot_nt(out_twice, in_twice)
    rows = lax.broadcasted_iota(jnp.int32, (pair, pair), 0) < rank
    cols = lax.broadcasted_iota(jnp.int32, (pair, pair), 1) < rank
    grads = jnp.where(rows == cols, grads, 0.0).astype(BF16)
    projected = jnp.dot(left, jnp.concatenate([grads, grads], axis=0), preferred_element_type=F32)
    projected = jnp.concatenate(split(projected), axis=1).astype(BF16)
    both = jnp.dot(projected, weights[...], preferred_element_type=F32)
    own[...] = (both[:, :pair] + both[:, pair:]).astype(BF16)

    sends = []

    def share(block, source, target):
        copy = pltpu.make_async_remote_copy(
            src_ref=block,
            dst_ref=gathered.at[source],
            send_sem=send_sem.at[len(sends)],
            recv_sem=recv_sem.at[source],
            device_id=(target, layer),
            device_id_type=MESH,
        )
        copy.start()
        sends.append(copy)

    def arrive(source):
        pltpu.make_async_remote_copy(
            src_ref=own,
            dst_ref=gathered.at[source],
            send_sem=send_sem.at[0],
            recv_sem=recv_sem.at[source],
            device_id=(sibling, layer),
            device_id_type=MESH,
        ).wait_recv()

    for peer in peers:
        share(own, me, peer)
    share(own, me, sibling)
    gathered[me] = own[...]
    for peer in peers:
        arrive(peer)
        share(gathered.at[peer], peer, sibling)
    train_load.wait()
    arrive(sibling)
    for k in range(1, n // 2):
        arrive(lax.rem(sibling + 2 * k, n))

    wide[...] = gathered[...].astype(F32).reshape(wide.shape)
    conditioned = jnp.concatenate(
        [wide[pl.ds(j, n, stride=half), :] for j in range(half)], axis=1
    ).astype(BF16)
    scores = dot_nt(conditioned, train[...])
    partial[...] = scores.reshape(partial.shape)
    layer_sends = []
    for k in range(1, m):
        copy = pltpu.make_async_remote_copy(
            src_ref=partial.at[layers[k - 1]],
            dst_ref=arrived.at[k],
            send_sem=layer_send_sem.at[k],
            recv_sem=layer_recv_sem.at[k],
            device_id=(me, layers[k - 1]),
            device_id_type=MESH,
        )
        copy.start()
        layer_sends.append(copy)
    total = partial[layer]
    for copy in sends:
        copy.wait_send()
    for k in range(1, m):
        layer_sends[k - 1].wait_recv()
        total = total + arrived[k]
    out_ref[...] = total
    for copy in layer_sends:
        copy.wait_send()


def body(n, m, *args):
    inputs, _, _, proj_in, _, _, _, train = args
    _, _, tokens, width = inputs.shape
    rank = proj_in.shape[1]
    count = train.shape[1]
    rows = n // m
    half, pair = rank // 2, 2 * rank
    hbm = pl.BlockSpec(memory_space=pltpu.HBM)
    return pl.pallas_call(
        functools.partial(kernel, n, m),
        out_shape=jax.ShapeDtypeStruct((rows, count), F32),
        in_specs=[hbm, hbm, pl.BlockSpec(memory_space=pltpu.SMEM)] + [hbm] * 5,
        out_specs=pl.BlockSpec(memory_space=pltpu.VMEM),
        scratch_shapes=[
            pltpu.VMEM((tokens, width), BF16),
            pltpu.VMEM((tokens, width), BF16),
            pltpu.VMEM((rank, width), BF16),
            pltpu.VMEM((rank, width), BF16),
            pltpu.VMEM((rank, rank), F32),
            pltpu.VMEM((rank, rank), F32),
            pltpu.VMEM((count, rank * rank), BF16),
            pltpu.VMEM((2 * pair, 2 * pair), BF16),
            pltpu.VMEM((half, pair), BF16),
            pltpu.VMEM((n, half, pair), BF16),
            pltpu.VMEM((n * half, pair), F32),
            pltpu.VMEM((m, rows, count), F32),
            pltpu.VMEM((m, rows, count), F32),
            pltpu.SemaphoreType.DMA((4, CHUNKS)),
            pltpu.SemaphoreType.DMA((4,)),
            pltpu.SemaphoreType.DMA((n,)),
            pltpu.SemaphoreType.DMA((n,)),
            pltpu.SemaphoreType.DMA((m,)),
            pltpu.SemaphoreType.DMA((m,)),
        ],
        compiler_params=pltpu.CompilerParams(
            collective_id=0, has_side_effects=True, vmem_limit_bytes=55212 * 1024
        ),
    )(*args)


def solution(mesh):
    n, m = mesh.shape["dp"], mesh.shape["layer"]
    in_specs = (
        P("layer", "dp", None, None),
        P("layer", "dp", None, None),
        P("dp"),
        P("layer", None, None),
        P("layer", None, None),
        P("layer", None, None),
        P("layer", None, None),
        P("layer", "dp", None),
    )
    return jax.shard_map(
        functools.partial(body, n, m),
        mesh=mesh,
        in_specs=in_specs,
        out_specs=P("layer", "dp"),
        check_vma=False,
    )
```
